128 devices in a mesh: outer: 8 (over y_lo, x), inner: 16 (over z, y_hi, core).
Axes of the slice: x: 4, y: 4 (y_hi: 2, y_lo: 2; y = y_hi * 2 + y_lo), z: 4, core: 2. Of those that a mesh axis runs over, the one named last changes fastest.
Arguments:
- queries: bfloat16 [16384, 1536], P(('outer', 'inner')), may hold values from -6.2 to 6.2
- keys: bfloat16 [16384, 128], P(('outer', 'inner')), may hold values from -4 to 4
- values: bfloat16 [16384, 128], P(('outer', 'inner')), may hold values from -6 to 6
- doc_lengths: int32 [16], replicated, may hold values from 1 to 8192, 16384 in all
Outputs:
- attended: bfloat16 [16384, 1536], P(('outer', 'inner'))
The draws below stay inside these ranges and needn't reach their ends.
Inputs may be any that keep to these rules, and one draw needn't show every extreme that they name: `doc_lengths`: 16 lengths summing to 16384; the longest is exactly 8192.
All inputs are finite; a program needn't handle non-finite values.
Results may differ from the reference program's by a relative error of at most 0.0059.
Values may be sent and summed in bfloat16 or wider, within the bound.
No kernel may reach another device: no remote copies, remote signals or barrier semaphores. Data moves between devices by JAX's collectives and lax.ppermute only.
A program may use at most 64 MiB of HBM per device.

```python
import math
import jax
import jax.numpy as jnp
import numpy as np
from jax import lax

HQ = 12
HD = 128
DOCS = 16
TOKENS = 16384
DOC_MAX = 8192


def draw_queries(key, part):
    key = jax.random.fold_in(key, 1)
    drawn = jnp.clip(2.0 * jax.random.normal(key, (TOKENS, HQ * HD), jnp.float32), -6.0, 6.0)
    return drawn.astype(jnp.bfloat16)


def draw_keys(key, part):
    key = jax.random.fold_in(key, 2)
    drawn = jnp.clip(jax.random.normal(key, (TOKENS, HD), jnp.float32), -4.0, 4.0)
    return drawn.astype(jnp.bfloat16)


def shard_levels(own_key, dims, shards, least, largest):
    loudness = 1.0
    for dim, blocks in shards:
        steps = jax.random.uniform(jax.random.fold_in(jax.random.fold_in(own_key, 6), dim), (blocks,), jnp.float32, least / len(shards), largest / len(shards))
        loudness = loudness * jnp.repeat(jnp.exp(steps), dims[dim] // blocks).reshape((-1,) + (1,) * (len(dims) - 1 - dim))
    return loudness


def profile(count, total, most, slope):
    weights = [(1 << 20) // math.isqrt(rank ** slope) + 1 for rank in range(2, count + 1)]
    surplus, holding = total - most - (count - 1), [1] * (count - 1)
    while surplus > 0:
        free = [i for i in range(count - 1) if holding[i] < most]
        whole, left = sum([weights[i] for i in free]), surplus
        for i in free:
            addition = min(most - holding[i], max(1, left * weights[i] // whole), surplus)
            holding[i] = holding[i] + addition
            surplus = surplus - addition
    return np.array([most] + holding)


def uneven_parts(stream_key, count, total, bound, slope):
    if count == 2:
        one = jax.random.randint(stream_key, (), max(1, total - bound), min(bound, total - 1) + 1)
        return jnp.stack([one, total - one])
    sizes = jnp.asarray(profile(count, total, bound, slope), jnp.int32)
    twos = (count - 1) // 2
    source_of, taker = sizes[1:1 + 2 * twos:2], sizes[2:2 + 2 * twos:2]
    margin = jnp.minimum(source_of - 1, bound - taker)
    shifted = jax.random.randint(jax.random.fold_in(stream_key, 1), (twos,), 0, 1 << 20) % (margin + 1)
    sizes = sizes.at[1:1 + 2 * twos:2].set(source_of - shifted).at[2:2 + 2 * twos:2].set(taker + shifted)
    return sizes[jax.random.permutation(jax.random.fold_in(stream_key, 2), count)]


def noise(stream_key, extent, scale, bound, cuts=(), kind=jnp.bfloat16):
    gain = shard_levels(stream_key, extent, cuts, -0.22, 0.18) if cuts else 1.0
    values = jax.random.normal(stream_key, extent, jnp.float32) * scale * gain
    return jnp.minimum(jnp.maximum(values, -bound), bound).astype(kind)


def setup_inputs(seed: int = 0) -> dict:
    arg_keys = jax.random.split(jax.random.key(seed), 5)
    queries = draw_queries(jax.random.fold_in(arg_keys[4], 71), 0)
    keys = draw_keys(jax.random.fold_in(arg_keys[4], 71), 0)
    values = noise(arg_keys[2], (TOKENS, HD), 1.0, 6.0, ((0, 128),))
    doc_lengths = uneven_parts(arg_keys[3], DOCS, TOKENS, DOC_MAX, 2).astype(jnp.int32)
    return {"queries": queries, "keys": keys, "values": values, "doc_lengths": doc_lengths}


def reference(queries, keys, values, doc_lengths):
    positions = jnp.arange(TOKENS, dtype=jnp.int32)
    ends = jnp.cumsum(doc_lengths).astype(jnp.int32)
    starts = jnp.max(jnp.where(ends[None, :] <= positions[:, None], ends[None, :], 0), axis=1).astype(jnp.int32)
    scale = HD ** -0.5
    stride_rows = 512
    pieces = []
    for block_index in range(TOKENS // stride_rows):
        first_row = block_index * stride_rows
        last_row = first_row + stride_rows
        query_block = queries[first_row:last_row].astype(jnp.float32).reshape(stride_rows, HQ, HD)
        key_block = keys[:last_row].astype(jnp.float32)
        value_block = values[:last_row].astype(jnp.float32)
        scores = jnp.einsum("qhd,kd->hqk", query_block, key_block, precision=lax.Precision.HIGHEST) * scale
        key_pos = positions[:last_row]
        allowed = (key_pos[None, :] >= starts[first_row:last_row, None]) & (key_pos[None, :] <= positions[first_row:last_row, None])
        scores = jnp.where(allowed[None], scores, -jnp.inf)
        highest = jnp.max(scores, axis=2, keepdims=True)
        weights = jnp.exp(scores - highest)
        total = jnp.sum(weights, axis=2)
        low_weights = lax.optimization_barrier(weights.astype(jnp.bfloat16)).astype(jnp.float32)
        summed = jnp.einsum("hqk,kd->hqd", low_weights, value_block, precision=lax.Precision.HIGHEST)
        result = summed / total[:, :, None]
        pieces.append(result.transpose(1, 0, 2).reshape(stride_rows, HQ * HD))
    return jnp.concatenate(pieces, axis=0).astype(jnp.bfloat16)
```

```python
import functools
import math

import jax
import jax.numpy as jnp
from jax import lax
from jax.experimental import pallas as pl
from jax.experimental.pallas import tpu as pltpu
from jax.sharding import PartitionSpec as P

AXES = ("outer", "inner")
HEADS = 12
SIZE = 128
BLOCK = 128
RUN = 64
SCALE = math.log2(math.e) / math.sqrt(SIZE)
MASKED = -1e30
EMPTY = -1e20
TILE_HEADS = 6


def number(x, y, z, core):
    return ((y % 2) * 4 + x) * 16 + z * 4 + (y // 2) * 2 + core


def swap(array, x=0, y=0, z=0, core=0):
    pairs = [
        (number(a, b, c, d), number(a ^ x, b ^ y, c ^ z, d ^ core))
        for a in range(4)
        for b in range(4)
        for c in range(4)
        for d in range(2)
    ]
    return lax.ppermute(array, AXES, pairs)


def place(device):
    return device // 64, (device // 16) % 4, (device // 4) % 4, (device // 2) % 2, device % 2


def flag(condition):
    return jnp.where(condition, 1, 0).astype(jnp.int32)


def attend(stage, step_runs, steps, tile_heads, *refs):
    refs = list(refs)
    device_ref, docs_ref, own_ref, other_ref = refs[:4]
    refs = refs[4:]
    if stage == "first":
        pieces, refs = refs[:7], refs[7:]
    else:
        pieces, refs = refs[:3], refs[3:]
    if stage != "first":
        accum_in, stat_in = refs[:2]
        refs = refs[2:]
    if stage == "last":
        own_out, own_stat, sent = refs[:3]
        refs = refs[3:]
    else:
        accum_out, stat_out = refs[:2]
        refs = refs[2:]
    rows, window, top, total, accum, bias, first_pos, query_pos, base_ref = refs
    keys_step = step_runs * RUN
    device = device_ref[0]
    half, x, z, g, core = place(device)
    chip = device // 2

    token = lax.broadcasted_iota(jnp.int32, (2 * BLOCK, 128), 0)
    position = jnp.where(
        token < BLOCK, device * BLOCK + token, (chip * 4 + 1 - device) * BLOCK + token - BLOCK
    )
    lowest, highest = chip * 2 * BLOCK, chip * 2 * BLOCK + 2 * BLOCK - 1
    start = jnp.zeros_like(position)
    low_start, high_start, end = jnp.int32(0), jnp.int32(0), jnp.int32(0)
    for j in range(docs_ref.shape[0]):
        end = end + docs_ref[j]
        start = jnp.where(position >= end, end, start)
        low_start = jnp.where(lowest >= end, end, low_start)
        high_start = jnp.where(highest >= end, end, high_start)
    query_pos[...] = position
    first_pos[...] = start

    def base(chosen, xs, zs, gs, piece):
        return ((chosen * 4 + xs) * 16 + zs * 4 + gs * 2 + core) * BLOCK + piece * RUN

    runs = []
    if stage == "first":
        own = pieces[0]
        for chosen in range(2):
            for r in range(2):
                for piece in range(2):
                    runs.append(
                        (
                            own[chosen, r, piece * RUN : (piece + 1) * RUN, :],
                            base(chosen, x, z, g ^ r, piece),
                        )
                    )
        for k in (1, 2, 3):
            chosen = half * flag((z ^ k) < z)
            for r in range(2):
                runs.append((pieces[k][chosen, r], base(chosen, x, z ^ k, g ^ r, 0)))
        for k in (1, 2, 3):
            chosen = half * flag((x ^ k) < x)
            for r in range(2):
                runs.append((pieces[3 + k][r], base(chosen, x ^ k, z, g ^ r, 1)))
    elif stage == "middle":
        for k in (1, 2, 3):
            chosen = half * flag((x ^ k) < x)
            for j in range(4):
                for r in range(2):
                    runs.append((pieces[k - 1][j, r], base(chosen, x ^ k, z ^ j, g ^ r, 0)))
    else:
        for k in (1, 2, 3):
            for j in range(4):
                chosen = half * (flag((x ^ j) < x) if j else flag((z ^ k) < z))
                for r in range(2):
                    runs.append((pieces[k - 1][j, r], base(chosen, x ^ j, z ^ k, g ^ r, 1)))
    for i, (values, begin) in enumerate(runs):
        window[i * RUN : (i + 1) * RUN, :] = values
        base_ref[i] = begin

    for h in range(HEADS):
        columns = slice(h * SIZE, (h + 1) * SIZE)
        rows[h * 256 : h * 256 + 128, :] = own_ref[:, columns]
        rows[h * 256 + 128 : h * 256 + 256, :] = other_ref[:, columns]
    if stage == "first":
        top[...] = jnp.full_like(top, EMPTY)
        total[...] = jnp.zeros_like(total)
        accum[...] = jnp.zeros_like(accum)
    else:
        accum[...] = accum_in[...]
        for h in range(HEADS):
            span = slice(h * 256, (h + 1) * 256)
            top[span, :] = jnp.broadcast_to(stat_in[:, h : h + 1], (256, 128))
            lane = lax.broadcasted_iota(jnp.int32, (256, 128), 1)
            held = jnp.broadcast_to(stat_in[:, 16 + h : 17 + h], (256, 128))
            total[span, :] = jnp.where(lane == 0, held, 0.0)

    size = tile_heads * 256

    def tile(t, offset, masked):
        span = pl.ds(pl.multiple_of(t * size, size), size)
        key = window[pl.ds(offset, keys_step), 0:128]
        value = window[pl.ds(offset, keys_step), 128:256]
        scores = lax.dot_general(
            rows[span, :], key, (((1,), (1,)), ((), ())), preferred_element_type=jnp.float32
        )
        if masked:
            scores = scores + jnp.concatenate([bias[...]] * tile_heads, axis=0)
        before = top[span, :]
        fresh = jnp.maximum(before, jnp.max(scores, axis=1, keepdims=True) * SCALE)
        weights = jnp.exp2(scores * SCALE - jnp.concatenate([fresh] * (keys_step // 128), axis=1))
        factor = jnp.exp2(before - fresh)
        part = weights[:, 0:128]
        for j in range(1, keys_step // 128):
            part = part + weights[:, j * 128 : (j + 1) * 128]
        total[span, :] = total[span, :] * factor + part
        accum[span, :] = accum[span, :] * factor + lax.dot_general(
            weights.astype(jnp.bfloat16),
            value,
            (((1,), (0,)), ((), ())),
            preferred_element_type=jnp.float32,
        )
        top[span, :] = fresh

    def step(i, carry):
        some, every = jnp.int32(0), jnp.int32(1)
        for j in range(step_runs):
            begin = base_ref[i * step_runs + j]
            some = some | flag((begin <= highest) & (begin + RUN - 1 >= low_start))
            every = every & flag((begin + RUN - 1 <= lowest) & (begin >= high_start))
        offset = pl.multiple_of(i * keys_step, keys_step)

        @pl.when((some == 1) & (every == 1))
        def _():
            for t in range(HEADS // tile_heads):
                tile(t, offset, False)

        @pl.when((some == 1) & (every == 0))
        def _():
            lane = lax.broadcasted_iota(jnp.int32, (2 * BLOCK, 128), 1)
            for j in range(step_runs // 2):
                left = base_ref[i * step_runs + 2 * j]
                right = base_ref[i * step_runs + 2 * j + 1] - RUN
                key_pos = lane + jnp.where(lane < RUN, left, right)
                allowed = (key_pos >= first_pos[...]) & (key_pos <= query_pos[...])
                bias[:, j * 128 : (j + 1) * 128] = jnp.where(allowed, 0.0, MASKED)
            for t in range(HEADS // tile_heads):
                tile(t, offset, True)

        return carry

    lax.fori_loop(0, steps, step, 0)

    lane = lax.broadcasted_iota(jnp.int32, (256, 128), 1)
    if stage != "last":
        accum_out[...] = accum[...]
        stat = jnp.zeros((256, 128), jnp.float32)
        for h in range(HEADS):
            span = slice(h * 256, (h + 1) * 256)
            stat = jnp.where(lane == h, top[span, :], stat)
            held = jnp.sum(total[span, :], axis=1, keepdims=True)
            stat = jnp.where(lane == 16 + h, held, stat)
        stat_out[...] = stat
        return
    stat = jnp.zeros((256, 128), jnp.float32)
    for h in range(HEADS):
        columns = slice(h * SIZE, (h + 1) * SIZE)
        span = slice(h * 256, (h + 1) * 256)
        held = jnp.sum(total[span, :], axis=1, keepdims=True)
        filled = held > 0.0
        divisor = jnp.where(filled, held, 1.0)
        level = jnp.where(filled, top[span, :] + jnp.log2(divisor), EMPTY)
        stat = jnp.where(lane == h, level, stat)
        result = accum[span, :] / divisor
        own_out[:, columns] = result[:128, :]
        sent[:, columns] = result[128:, :].astype(jnp.bfloat16)
    own_stat[...] = stat[:128, :]
    rest = stat[128:, :]
    high = rest.astype(jnp.bfloat16)
    rest = rest - high.astype(jnp.float32)
    middle = rest.astype(jnp.bfloat16)
    low = (rest - middle.astype(jnp.float32)).astype(jnp.bfloat16)
    base_column = HEADS * SIZE
    sent[:, base_column : base_column + 128] = high
    sent[:, base_column + 128 : base_column + 256] = middle
    sent[:, base_column + 256 : base_column + 384] = low


def merge(own_ref, stat_ref, got_ref, out_ref):
    base_column = HEADS * SIZE
    other = (
        got_ref[:, base_column : base_column + 128].astype(jnp.float32)
        + got_ref[:, base_column + 128 : base_column + 256].astype(jnp.float32)
    ) + got_ref[:, base_column + 256 : base_column + 384].astype(jnp.float32)
    mine = stat_ref[...]
    peak = jnp.maximum(mine, other)
    left, right = jnp.exp2(mine - peak), jnp.exp2(other - peak)
    both = left + right
    left, right = left / both, right / both
    for h in range(HEADS):
        columns = slice(h * SIZE, (h + 1) * SIZE)
        out_ref[:, columns] = (
            own_ref[:, columns] * left[:, h : h + 1]
            + got_ref[:, columns].astype(jnp.float32) * right[:, h : h + 1]
        ).astype(jnp.bfloat16)


def call(stage, step_runs, steps, device, doc_lengths, own, other, pieces, state):
    smem = pl.BlockSpec(memory_space=pltpu.SMEM)
    vmem = pl.BlockSpec(memory_space=pltpu.VMEM)
    tokens = 2 * BLOCK
    rows = HEADS * tokens
    if stage == "last":
        out_shape = (
            jax.ShapeDtypeStruct((BLOCK, HEADS * SIZE), jnp.float32),
            jax.ShapeDtypeStruct((BLOCK, 128), jnp.float32),
            jax.ShapeDtypeStruct((BLOCK, HEADS * SIZE + 384), jnp.bfloat16),
        )
    else:
        out_shape = (
            jax.ShapeDtypeStruct((rows, SIZE), jnp.float32),
            jax.ShapeDtypeStruct((tokens, 128), jnp.float32),
        )
    keys = steps * step_runs * RUN
    return pl.pallas_call(
        functools.partial(attend, stage, step_runs, steps, TILE_HEADS),
        out_shape=out_shape,
        in_specs=[smem, smem] + [vmem] * (2 + len(pieces) + len(state)),
        out_specs=(vmem,) * len(out_shape),
        scratch_shapes=[
            pltpu.VMEM((rows, SIZE), jnp.bfloat16),
            pltpu.VMEM((keys, 2 * SIZE), jnp.bfloat16),
            pltpu.VMEM((rows, 128), jnp.float32),
            pltpu.VMEM((rows, 128), jnp.float32),
            pltpu.VMEM((rows, 128), jnp.float32),
            pltpu.VMEM((tokens, step_runs * RUN), jnp.float32),
            pltpu.VMEM((tokens, 128), jnp.int32),
            pltpu.VMEM((tokens, 128), jnp.int32),
            pltpu.SMEM((steps * step_runs,), jnp.int32),
        ],
        compiler_params=pltpu.CompilerParams(vmem_limit_bytes=48 * 2**20),
        cost_estimate=pl.CostEstimate(
            flops=4 * rows * keys * SIZE, bytes_accessed=4 * 2**20, transcendentals=rows * keys
        ),
    )(device, doc_lengths, own, other, *pieces, *state)


def body(queries, keys, values, doc_lengths):
    device = lax.axis_index(AXES).astype(jnp.int32)
    half, x, z, g, core = place(device)
    pair = jnp.concatenate([keys, values], axis=1)
    across = swap(pair, y=1)
    other = swap(queries, core=1)
    both = jnp.stack([jnp.where(half == 0, pair, across), jnp.where(half == 0, across, pair)])
    plane = jnp.stack([both, swap(both, y=3)], axis=1)
    upper, lower = plane[:, :, :RUN], plane[:, :, RUN:]

    def pick(array, axis, second):
        return jnp.where(
            second,
            lax.index_in_dim(array, 1, axis, False),
            lax.index_in_dim(array, 0, axis, False),
        )

    later = half == 1
    order = (1, 3, 2)
    up_z = {k: swap(upper, z=k) for k in order}
    low_x = {k: swap(pick(lower, 0, later & ((x ^ k) > x)), x=k) for k in order}
    stacked = jnp.stack([upper] + [up_z[k] for k in (1, 2, 3)])
    up_x = {k: swap(pick(stacked, 1, later & ((x ^ k) > x)), x=k) for k in order}
    rest = [low_x[k] for k in (1, 2, 3)]
    low_z = {
        k: swap(jnp.stack([pick(lower, 0, later & ((z ^ k) > z))] + rest), z=k) for k in order
    }
    where = device.reshape(1)
    state = call(
        "first",
        10,
        2,
        where,
        doc_lengths,
        queries,
        other,
        [plane] + [up_z[k] for k in (1, 2, 3)] + rest,
        (),
    )
    state = call(
        "middle", 8, 3, where, doc_lengths, queries, other, [up_x[k] for k in (1, 2, 3)], state
    )
    own, stat, sent = call(
        "last", 8, 3, where, doc_lengths, queries, other, [low_z[k] for k in (1, 2, 3)], state
    )
    got = swap(sent, core=1)
    vmem = pl.BlockSpec(memory_space=pltpu.VMEM)
    return pl.pallas_call(
        merge,
        out_shape=jax.ShapeDtypeStruct(queries.shape, jnp.bfloat16),
        in_specs=[vmem] * 3,
        out_specs=vmem,
    )(own, stat, got)


def solution(mesh):
    in_specs = (P(AXES, None), P(AXES, None), P(AXES, None), P())
    return jax.shard_map(
        body, mesh=mesh, in_specs=in_specs, out_specs=P(AXES, None), check_vma=False
    )
```

```python
import functools
import math

import jax
import jax.numpy as jnp
from jax import lax
from jax.experimental import pallas as pl
from jax.experimental.pallas import tpu as pltpu
from jax.sharding import PartitionSpec as P

AXES = ("outer", "inner")
HEADS = 12
SIZE = 128
BLOCK = 128
SCALE = math.log2(math.e) / math.sqrt(SIZE)
MASKED = -1e30
EMPTY = -1e20
STEP = 4


def number(x, y, z, core):
    return ((y % 2) * 4 + x) * 16 + z * 4 + (y // 2) * 2 + core


def swap(array, partner):
    pairs = [
        (number(a, b, c, d), number(*partner(a, b, c, d)))
        for a in range(4)
        for b in range(4)
        for c in range(4)
        for d in range(2)
    ]
    return lax.ppermute(array, AXES, pairs)


def place(device):
    return device // 64, (device // 16) % 4, (device // 4) % 4, (device // 2) % 2, device % 2


def flag(condition):
    return jnp.where(condition, 1, 0).astype(jnp.int32)


def attend(stage, *refs):
    refs = list(refs)
    device_ref, docs_ref = refs[:2]
    refs = refs[2:]
    count = {"first": 4, "middle": 1, "last": 2}[stage]
    if stage == "first":
        own_ref, other_ref = refs[:2]
        pieces, refs = refs[2 : 2 + count], refs[2 + count :]
        rows, first_pos, query_pos, top, total, accum = refs[:6]
        refs = refs[6:]
    else:
        pieces, refs = refs[:count], refs[count:]
        rows, first_pos, query_pos, top_in, total_in, accum_in = refs[:6]
        refs = refs[6:]
        if stage == "last":
            own_out, own_stat, sent, top, total, accum = refs[:6]
            refs = refs[6:]
        else:
            top, total, accum = refs[:3]
            refs = refs[3:]
    window, bias, base_ref = refs
    device = device_ref[0]
    half, x, z, g, core = place(device)
    chip = device // 2

    lowest, highest = chip * 2 * BLOCK, chip * 2 * BLOCK + 2 * BLOCK - 1
    low_start, high_start, end = jnp.int32(0), jnp.int32(0), jnp.int32(0)
    ends = []
    for j in range(docs_ref.shape[0]):
        end = end + docs_ref[j]
        ends.append(end)
        low_start = jnp.where(lowest >= end, end, low_start)
        high_start = jnp.where(highest >= end, end, high_start)
    if stage == "first":
        token = lax.broadcasted_iota(jnp.int32, (2 * BLOCK, 128), 0)
        position = jnp.where(
            token < BLOCK, device * BLOCK + token, (chip * 4 + 1 - device) * BLOCK + token - BLOCK
        )
        start = jnp.zeros_like(position)
        for end in ends:
            start = jnp.where(position >= end, end, start)
        query_pos[...] = position
        first_pos[...] = start
        for h in range(HEADS):
            columns = slice(h * SIZE, (h + 1) * SIZE)
            rows[h * 256 : h * 256 + 128, :] = own_ref[:, columns]
            rows[h * 256 + 128 : h * 256 + 256, :] = other_ref[:, columns]
        top[...] = jnp.full_like(top, EMPTY)
        total[...] = jnp.zeros_like(total)
        accum[...] = jnp.zeros_like(accum)
    else:
        top[...] = top_in[...]
        total[...] = total_in[...]
        accum[...] = accum_in[...]

    def base(chosen, xs, zs, gs):
        return ((chosen * 4 + xs) * 16 + zs * 4 + gs * 2 + core) * BLOCK

    blocks = []
    if stage == "first":
        own = pieces[0]
        chosen = half * flag((g ^ 1) < g)
        blocks.append((own[half, 0], base(half, x, z, g)))
        blocks.append((own[chosen, 1], base(chosen, x, z, g ^ 1)))
        for k in (1, 2, 3):
            xs, zs = jnp.where(core == 0, x, x ^ k), jnp.where(core == 0, z ^ k, z)
            chosen = half * flag(xs * 4 + zs < x * 4 + z)
            for r in range(2):
                blocks.append((pieces[k][chosen, r], base(chosen, xs, zs, g ^ r)))
        blocks.append((own[1 - half, 0], base(1 - half, x, z, g)))
    else:
        for k, piece in zip((1,) if stage == "middle" else (3, 2), pieces, strict=True):
            for j in range(4):
                xs = jnp.where(core == 0, x ^ k, x ^ j)
                zs = jnp.where(core == 0, z ^ j, z ^ k)
                chosen = half * flag(xs * 4 + zs < x * 4 + z)
                for r in range(2):
                    blocks.append((piece[j, r], base(chosen, xs, zs, g ^ r)))
    for i, (values, begin) in enumerate(blocks):
        window[i * BLOCK : (i + 1) * BLOCK, :] = values
        base_ref[i] = begin

    def tile(offset, width, masked):
        key = window[pl.ds(offset, width), 0:128]
        value = window[pl.ds(offset, width), 128:256]
        scores = lax.dot_general(
            rows[...], key, (((1,), (1,)), ((), ())), preferred_element_type=jnp.float32
        )
        if masked:
            scores = scores + jnp.concatenate([bias[:, :width]] * HEADS, axis=0)
        before = top[...]
        fresh = jnp.maximum(before, jnp.max(scores, axis=1, keepdims=True) * SCALE)
        weights = jnp.exp2(scores * SCALE - jnp.concatenate([fresh] * (width // 128), axis=1))
        factor = jnp.exp2(before - fresh)
        part = weights[:, 0:128]
        for j in range(1, width // 128):
            part = part + weights[:, j * 128 : (j + 1) * 128]
        total[...] = total[...] * factor + part
        accum[...] = accum[...] * factor + lax.dot_general(
            weights.astype(jnp.bfloat16),
            value,
            (((1,), (0,)), ((), ())),
            preferred_element_type=jnp.float32,
        )
        top[...] = fresh

    def step(first, count):
        some, every = jnp.int32(0), jnp.int32(1)
        for j in range(count):
            begin = base_ref[first + j]
            some = some | flag((begin <= highest) & (begin + BLOCK - 1 >= low_start))
            every = every & flag((begin + BLOCK - 1 <= lowest) & (begin >= high_start))
        offset = first * BLOCK
        if not isinstance(first, int):
            offset = pl.multiple_of(offset, BLOCK)

        @pl.when((some == 1) & (every == 1))
        def _():
            tile(offset, count * BLOCK, False)

        @pl.when((some == 1) & (every == 0))
        def _():
            lane = lax.broadcasted_iota(jnp.int32, (2 * BLOCK, 128), 1)
            for j in range(count):
                key_pos = lane + base_ref[first + j]
                allowed = (key_pos >= first_pos[...]) & (key_pos <= query_pos[...])
                bias[:, j * 128 : (j + 1) * 128] = jnp.where(allowed, 0.0, MASKED)
            tile(offset, count * BLOCK, True)

    def advance(i, carry):
        step(i * STEP, STEP)
        return carry

    lax.fori_loop(0, len(blocks) // STEP, advance, 0)
    if len(blocks) % STEP:
        step(len(blocks) - 1, 1)

    if stage != "last":
        return
    lane = lax.broadcasted_iota(jnp.int32, (256, 128), 1)
    stat = jnp.zeros((256, 128), jnp.float32)
    for h in range(HEADS):
        columns = slice(h * SIZE, (h + 1) * SIZE)
        span = slice(h * 256, (h + 1) * 256)
        held = jnp.sum(total[span, :], axis=1, keepdims=True)
        filled = held > 0.0
        divisor = jnp.where(filled, held, 1.0)
        level = jnp.where(filled, top[span, :] + jnp.log2(divisor), EMPTY)
        stat = jnp.where(lane == h, level, stat)
        result = accum[span, :] / divisor
        own_out[:, columns] = result[:128, :]
        sent[:, columns] = result[128:, :].astype(jnp.bfloat16)
    own_stat[...] = stat[:128, :]
    rest = stat[128:, :]
    high = rest.astype(jnp.bfloat16)
    rest = rest - high.astype(jnp.float32)
    middle = rest.astype(jnp.bfloat16)
    low = (rest - middle.astype(jnp.float32)).astype(jnp.bfloat16)
    base_column = HEADS * SIZE
    sent[:, base_column : base_column + 128] = high
    sent[:, base_column + 128 : base_column + 256] = middle
    sent[:, base_column + 256 : base_column + 384] = low


def merge(own_ref, stat_ref, got_ref, out_ref):
    base_column = HEADS * SIZE
    other = (
        got_ref[:, base_column : base_column + 128].astype(jnp.float32)
        + got_ref[:, base_column + 128 : base_column + 256].astype(jnp.float32)
    ) + got_ref[:, base_column + 256 : base_column + 384].astype(jnp.float32)
    mine = stat_ref[...]
    peak = jnp.maximum(mine, other)
    left, right = jnp.exp2(mine - peak), jnp.exp2(other - peak)
    both = left + right
    left, right = left / both, right / both
    for h in range(HEADS):
        columns = slice(h * SIZE, (h + 1) * SIZE)
        out_ref[:, columns] = (
            own_ref[:, columns] * left[:, h : h + 1]
            + got_ref[:, columns].astype(jnp.float32) * right[:, h : h + 1]
        ).astype(jnp.bfloat16)


def call(stage, device, doc_lengths, arrays, state):
    smem = pl.BlockSpec(memory_space=pltpu.SMEM)
    vmem = pl.BlockSpec(memory_space=pltpu.VMEM)
    tokens = 2 * BLOCK
    rows = HEADS * tokens
    shape = jax.ShapeDtypeStruct
    sums = (shape((rows, SIZE), jnp.float32),) * 3
    blocks = {"first": 9, "middle": 8, "last": 16}[stage]
    aliases = {}
    if stage == "first":
        out_shape = (
            shape((rows, SIZE), jnp.bfloat16),
            shape((tokens, 128), jnp.int32),
            shape((tokens, 128), jnp.int32),
        ) + sums
    else:
        out_shape = sums
        if stage == "last":
            out_shape = (
                shape((BLOCK, HEADS * SIZE), jnp.float32),
                shape((BLOCK, 128), jnp.float32),
                shape((BLOCK, HEADS * SIZE + 384), jnp.bfloat16),
            ) + sums
        held = 2 + len(arrays) + 3
        aliases = {held + i: len(out_shape) - 3 + i for i in range(3)}
    keys = blocks * BLOCK
    return pl.pallas_call(
        functools.partial(attend, stage),
        out_shape=out_shape,
        in_specs=[smem, smem] + [vmem] * (len(arrays) + len(state)),
        out_specs=(vmem,) * len(out_shape),
        scratch_shapes=[
            pltpu.VMEM((keys, 2 * SIZE), jnp.bfloat16),
            pltpu.VMEM((tokens, STEP * BLOCK), jnp.float32),
            pltpu.SMEM((blocks,), jnp.int32),
        ],
        input_output_aliases=aliases,
        compiler_params=pltpu.CompilerParams(vmem_limit_bytes=40 * 2**20),
        cost_estimate=pl.CostEstimate(
            flops=4 * rows * keys * SIZE, bytes_accessed=4 * 2**20, transcendentals=rows * keys
        ),
    )(device, doc_lengths, *arrays, *state)


def body(queries, keys, values, doc_lengths):
    device = lax.axis_index(AXES).astype(jnp.int32)
    half, x, z, g, core = place(device)
    pair = jnp.pad(keys, ((0, 0), (0, SIZE))) + jnp.pad(values, ((0, 0), (SIZE, 0)))
    across = swap(pair, lambda x, y, z, c: (x, y ^ 1, z, c))
    other = swap(queries, lambda x, y, z, c: (x, y, z, 1 - c))
    both = jnp.stack([jnp.where(half == 0, pair, across), jnp.where(half == 0, across, pair)])
    far = swap(both, lambda x, y, z, c: (x, y ^ 3, z, c))
    plane = jnp.stack([both, far], axis=1)

    def along(array, k, second):
        return swap(
            array,
            lambda x, y, z, c: (x ^ k, y, z, c) if (c == 1) != second else (x, y, z ^ k, c),
        )

    order = (1, 3, 2)
    near = {k: along(plane, k, False) for k in order}
    line = [plane] + [near[k] for k in (1, 2, 3)]
    pieces = {}
    for k in order:
        chosen = []
        for j in range(4):
            xr, zr = jnp.where(core == 0, x ^ k, x), jnp.where(core == 0, z, z ^ k)
            xs, zs = jnp.where(core == 0, x, x ^ j), jnp.where(core == 0, z ^ j, z)
            second = (half == 1) & (xs * 4 + zs < xr * 4 + zr)
            chosen.append(jnp.where(second, line[j][1], line[j][0]))
        pieces[k] = along(jnp.stack(chosen), k, True)
    where = device.reshape(1)
    rows, first_pos, query_pos, *sums = call(
        "first", where, doc_lengths, [queries, other] + line, ()
    )
    fixed = [rows, first_pos, query_pos]
    sums = call("middle", where, doc_lengths, [pieces[1]], fixed + list(sums))
    own, stat, sent, *_ = call(
        "last", where, doc_lengths, [pieces[3], pieces[2]], fixed + list(sums)
    )
    got = swap(sent, lambda x, y, z, c: (x, y, z, 1 - c))
    vmem = pl.BlockSpec(memory_space=pltpu.VMEM)
    return pl.pallas_call(
        merge,
        out_shape=jax.ShapeDtypeStruct(queries.shape, jnp.bfloat16),
        in_specs=[vmem] * 3,
        out_specs=vmem,
    )(own, stat, got)


def solution(mesh):
    in_specs = (P(AXES, None), P(AXES, None), P(AXES, None), P())
    return jax.shard_map(
        body, mesh=mesh, in_specs=in_specs, out_specs=P(AXES, None), check_vma=False
    )
```

```python
import functools
import math

import jax
import jax.numpy as jnp
from jax import lax
from jax.experimental import pallas as pl
from jax.experimental.pallas import tpu as pltpu
from jax.sharding import PartitionSpec as P

AXES = ("outer", "inner")
HEADS = 12
SIZE = 128
BLOCK = 128
SCALE = math.log2(math.e) / math.sqrt(SIZE)
MASKED = -1e30
EMPTY = -1e20
LEAST = 2.0**-80
MOST = 2.0**100
AFTER = 1 << 20
SIDES = 1
STEP = 4


def number(x, y, z, core):
    return ((y % 2) * 4 + x) * 16 + z * 4 + (y // 2) * 2 + core


def swap(array, partner):
    pairs = [
        (number(a, b, c, d), number(*partner(a, b, c, d)))
        for a in range(4)
        for b in range(4)
        for c in range(4)
        for d in range(2)
    ]
    return lax.ppermute(array, AXES, pairs)


def place(device):
    return device // 64, (device // 16) % 4, (device // 4) % 4, (device // 2) % 2, device % 2


def flag(condition):
    return jnp.where(condition, 1, 0).astype(jnp.int32)


def prepare(device_ref, docs_ref, queries_ref, unused_ref, rows, first_pos, query_pos):
    device = device_ref[0]
    chip = device // 2
    for h in range(HEADS):
        rows[h * BLOCK : (h + 1) * BLOCK, :] = queries_ref[:, h * SIZE : (h + 1) * SIZE]
    token = lax.broadcasted_iota(jnp.int32, (2 * BLOCK, 128), 0)
    position = jnp.where(
        token < BLOCK, device * BLOCK + token, (chip * 4 + 1 - device) * BLOCK + token - BLOCK
    )
    start = jnp.zeros_like(position)
    end = jnp.int32(0)
    for j in range(docs_ref.shape[0]):
        end = end + docs_ref[j]
        start = jnp.where(position >= end, end, start)
    query_pos[...] = position
    first_pos[...] = start


def blocks_of(stage, pieces, spot):
    half, x, z, g, core = spot

    def base(chosen, xs, zs, gs):
        return ((chosen * 4 + xs) * 16 + zs * 4 + gs * 2 + core) * BLOCK

    blocks = []
    if stage == "first":
        own = pieces[0]
        chosen = half * flag((g ^ 1) < g)
        blocks.append((own[half, 0], base(half, x, z, g)))
        blocks.append((own[chosen, 1], base(chosen, x, z, g ^ 1)))
        for k in (1, 2, 3):
            xs, zs = jnp.where(core == 0, x, x ^ k), jnp.where(core == 0, z ^ k, z)
            chosen = half * flag(xs * 4 + zs < x * 4 + z)
            for r in range(2):
                blocks.append((pieces[k][chosen, r], base(chosen, xs, zs, g ^ r)))
        blocks.append((own[1 - half, 0], base(1 - half, x, z, g)))
        return blocks
    for k, piece in zip((1,) if stage == "middle" else (3, 2), pieces, strict=True):
        for j in range(4):
            xs = jnp.where(core == 0, x ^ k, x ^ j)
            zs = jnp.where(core == 0, z ^ j, z ^ k)
            chosen = half * flag(xs * 4 + zs < x * 4 + z)
            for r in range(2):
                blocks.append((piece[j, r], base(chosen, xs, zs, g ^ r)))
    return blocks


def attend(stage, *refs):
    refs = list(refs)
    device_ref, docs_ref, first_pos, query_pos = refs[:4]
    refs = refs[4:]
    if stage == "first":
        own_ref, other_ref = refs[:2]
        pieces, refs = refs[2:6], refs[6:]
        rows, total, accum = refs[:3]
        window, bias, base_ref = refs[3:]
    else:
        rows, total_in, accum_in = refs[:3]
        refs = refs[3:]
        count = {"middle": 1, "last": 7}[stage]
        pieces, refs = refs[:count], refs[count:]
        if stage == "last":
            own_out, own_stat, sent = refs[:3]
            refs = refs[3:]
        total, accum = refs[:2]
        window, bias, base_ref = refs[2:5]
    device = device_ref[0]
    spot = place(device)
    chip = device // 2

    lowest, highest = chip * 2 * BLOCK, chip * 2 * BLOCK + 2 * BLOCK - 1
    low_start, high_start, end = jnp.int32(0), jnp.int32(0), jnp.int32(0)
    for j in range(docs_ref.shape[0]):
        end = end + docs_ref[j]
        low_start = jnp.where(lowest >= end, end, low_start)
        high_start = jnp.where(highest >= end, end, high_start)
    if stage == "first":
        rows[: HEADS * BLOCK, :] = own_ref[...]
        rows[HEADS * BLOCK :, :] = other_ref[...]

    def fill(blocks):
        for i, (values, begin) in enumerate(blocks):
            window[i * BLOCK : (i + 1) * BLOCK, :] = values
            base_ref[i] = begin

    def needed(first, count):
        some, every = jnp.int32(0), jnp.int32(1)
        for j in range(count):
            begin = base_ref[first + j]
            some = some | flag((begin <= highest) & (begin + BLOCK - 1 >= low_start))
            every = every & flag((begin + BLOCK - 1 <= lowest) & (begin >= high_start))
        return some, every

    def mask(first, count):
        lane = lax.broadcasted_iota(jnp.int32, (2 * BLOCK, 128), 1)
        for j in range(count):
            key_pos = lane + base_ref[first + j]
            allowed = (key_pos >= first_pos[...]) & (key_pos <= query_pos[...])
            bias[:, j * 128 : (j + 1) * 128] = jnp.where(allowed, 0.0, MASKED)

    def offset_of(first):
        return first * BLOCK if isinstance(first, int) else pl.multiple_of(first * BLOCK, BLOCK)

    def tile(first, count, masked, initial):
        width = count * BLOCK
        key = window[pl.ds(offset_of(first), width), 0:128]
        value = window[pl.ds(offset_of(first), width), 128:256]
        for side in range(SIDES):
            size = 2 * HEADS * BLOCK // SIDES
            span = slice(side * size, (side + 1) * size)
            scores = lax.dot_general(
                rows[span, :], key, (((1,), (1,)), ((), ())), preferred_element_type=jnp.float32
            )
            scores = scores * SCALE
            if masked:
                left, right = bias[:BLOCK, :width], bias[BLOCK:, :width]
                spread = ([left] * HEADS + [right] * HEADS)[
                    span.start // BLOCK : span.stop // BLOCK
                ]
                scores = scores + jnp.concatenate(spread, axis=0)
            weights = jnp.exp2(scores)
            part = weights[:, 0:128]
            for j in range(1, count):
                part = part + weights[:, j * 128 : (j + 1) * 128]
            product = jnp.dot(
                weights.astype(jnp.bfloat16), value, preferred_element_type=jnp.float32
            )
            if not initial:
                total[span, :] = total[span, :] + part
                accum[span, :] = accum[span, :] + product
            elif stage == "first":
                total[span, :] = part
                accum[span, :] = product
            else:
                total[span, :] = total_in[span, :] + part
                accum[span, :] = accum_in[span, :] + product

    def step(first, count, initial):
        some, every = needed(first, count)

        @pl.when((some == 1) & (every == 1))
        def _():
            tile(first, count, False, initial)

        @pl.when((some == 1) & (every == 0))
        def _():
            mask(first, count)
            tile(first, count, True, initial)

        if initial:

            @pl.when(some == 0)
            def _():
                if stage == "first":
                    total[...] = jnp.zeros_like(total)
                    accum[...] = jnp.zeros_like(accum)
                else:
                    total[...] = total_in[...]
                    accum[...] = accum_in[...]

    def advance(i, carry):
        step(i * STEP, STEP, False)
        return carry

    blocks = blocks_of(stage, pieces[:2] if stage == "last" else pieces, spot)
    fill(blocks)
    step(0, STEP, True)
    lax.fori_loop(1, len(blocks) // STEP, advance, 0)
    if len(blocks) % STEP:
        step(len(blocks) - 1, 1, False)
    if stage != "last":
        return

    top = refs[5]

    def finish(shifted):
        lane = lax.broadcasted_iota(jnp.int32, (BLOCK, 128), 1)
        bad = jnp.zeros((BLOCK, 1), jnp.int32)
        stats = []
        for side in range(2):
            stat = jnp.zeros((BLOCK, 128), jnp.float32)
            for h in range(HEADS):
                columns = slice(h * SIZE, (h + 1) * SIZE)
                span = slice((side * HEADS + h) * BLOCK, (side * HEADS + h + 1) * BLOCK)
                held = jnp.sum(total[span, :], axis=1, keepdims=True)
                fine = (held >= LEAST) & (held <= MOST)
                if side == 1:
                    fine = fine | (first_pos[BLOCK:, 0:1] >= (chip * 4 + 1 - device) * BLOCK)
                bad = jnp.where(fine, bad, 1)
                filled = held > 0.0
                divisor = jnp.where(filled, held, 1.0)
                level = jnp.log2(divisor)
                if shifted:
                    level = level + top[span, :]
                stat = jnp.where(lane == h, jnp.where(filled, level, EMPTY), stat)
                result = accum[span, :] * (1.0 / divisor)
                if side == 0:
                    own_out[:, columns] = result
                else:
                    sent[:, columns] = result.astype(jnp.bfloat16)
            stats.append(stat)
        own_stat[...] = stats[0]
        rest = stats[1]
        high = rest.astype(jnp.bfloat16)
        rest = rest - high.astype(jnp.float32)
        middle = rest.astype(jnp.bfloat16)
        low = (rest - middle.astype(jnp.float32)).astype(jnp.bfloat16)
        base_column = HEADS * SIZE
        sent[:, base_column : base_column + 128] = high
        sent[:, base_column + 128 : base_column + 256] = middle
        sent[:, base_column + 256 : base_column + 384] = low
        return jnp.max(bad)

    bad = finish(False)

    @pl.when(bad > 0)
    def _():
        top[...] = jnp.full_like(top, EMPTY)
        total[...] = jnp.zeros_like(total)
        accum[...] = jnp.zeros_like(accum)
        width = STEP * BLOCK

        def careful(i, carry):
            first = i * STEP
            mask(first, STEP)
            key = window[pl.ds(offset_of(first), width), 0:128]
            value = window[pl.ds(offset_of(first), width), 128:256]

            def head(t, carry):
                span = pl.ds(pl.multiple_of(t * BLOCK, BLOCK), BLOCK)
                side = pl.ds(pl.multiple_of(t // HEADS * BLOCK, BLOCK), BLOCK)
                scores = lax.dot_general(
                    rows[span, :],
                    key,
                    (((1,), (1,)), ((), ())),
                    preferred_element_type=jnp.float32,
                )
                scores = scores * SCALE + bias[side, :width]
                before = top[span, :]
                fresh = jnp.maximum(before, jnp.max(scores, axis=1, keepdims=True))
                weights = jnp.exp2(scores - jnp.concatenate([fresh] * STEP, axis=1))
                part = weights[:, 0:128]
                for j in range(1, STEP):
                    part = part + weights[:, j * 128 : (j + 1) * 128]
                factor = jnp.exp2(before - fresh)
                total[span, :] = total[span, :] * factor + part
                accum[span, :] = accum[span, :] * factor + jnp.dot(
                    weights.astype(jnp.bfloat16), value, preferred_element_type=jnp.float32
                )
                top[span, :] = fresh
                return carry

            lax.fori_loop(0, 2 * HEADS, head, 0)
            return carry

        for name, group in (("first", pieces[3:7]), ("middle", pieces[2:3]), ("last", pieces[:2])):
            again = blocks_of(name, group, spot)
            while len(again) % STEP:
                again.append((again[0][0], jnp.int32(AFTER)))
            fill(again)
            lax.fori_loop(0, len(again) // STEP, careful, 0)
        finish(True)


def merge(own_ref, stat_ref, got_ref, out_ref):
    base_column = HEADS * SIZE
    other = (
        got_ref[:, base_column : base_column + 128].astype(jnp.float32)
        + got_ref[:, base_column + 128 : base_column + 256].astype(jnp.float32)
    ) + got_ref[:, base_column + 256 : base_column + 384].astype(jnp.float32)
    mine = stat_ref[...]
    peak = jnp.maximum(mine, other)
    left, right = jnp.exp2(mine - peak), jnp.exp2(other - peak)
    both = left + right
    left, right = left / both, right / both
    for h in range(HEADS):
        columns = slice(h * SIZE, (h + 1) * SIZE)
        out_ref[:, columns] = (
            own_ref[:, columns] * left[:, h : h + 1]
            + got_ref[:, columns].astype(jnp.float32) * right[:, h : h + 1]
        ).astype(jnp.bfloat16)


def call(stage, scalars, arrays, pieces):
    smem = pl.BlockSpec(memory_space=pltpu.SMEM)
    vmem = pl.BlockSpec(memory_space=pltpu.VMEM)
    tokens = 2 * BLOCK
    rows = HEADS * tokens
    shape = jax.ShapeDtypeStruct
    out_shape = (shape((rows, SIZE), jnp.float32),) * 2
    blocks = {"first": 9, "middle": 8, "last": 16}[stage]
    scratch_shapes = [
        pltpu.VMEM((blocks * BLOCK, 2 * SIZE), jnp.bfloat16),
        pltpu.VMEM((tokens, STEP * BLOCK), jnp.float32),
        pltpu.SMEM((blocks,), jnp.int32),
    ]
    aliases = {}
    if stage == "first":
        out_shape = (shape((rows, SIZE), jnp.bfloat16),) + out_shape
    elif stage == "middle":
        aliases = {5: 0, 6: 1}
    else:
        out_shape = (
            shape((BLOCK, HEADS * SIZE), jnp.float32),
            shape((BLOCK, 128), jnp.float32),
            shape((BLOCK, HEADS * SIZE + 384), jnp.bfloat16),
        ) + out_shape
        aliases = {5: 3, 6: 4}
        scratch_shapes.append(pltpu.VMEM((rows, 128), jnp.float32))
    work = rows * blocks * BLOCK
    return pl.pallas_call(
        functools.partial(attend, stage),
        out_shape=out_shape,
        in_specs=[smem, smem] + [vmem] * (2 + len(arrays) + len(pieces)),
        out_specs=(vmem,) * len(out_shape),
        scratch_shapes=scratch_shapes,
        input_output_aliases=aliases,
        compiler_params=pltpu.CompilerParams(vmem_limit_bytes=40 * 2**20),
        cost_estimate=pl.CostEstimate(
            flops=4 * work * SIZE, bytes_accessed=4 * 2**20, transcendentals=work
        ),
    )(*scalars, *arrays, *pieces)


def body(queries, keys, values, doc_lengths):
    device = lax.axis_index(AXES).astype(jnp.int32)
    half, x, z, g, core = place(device)
    pair = jnp.pad(keys, ((0, 0), (0, SIZE))) + jnp.pad(values, ((0, 0), (SIZE, 0)))
    across = swap(pair, lambda x, y, z, c: (x, y ^ 1, z, c))
    both = jnp.stack([jnp.where(half == 0, pair, across), jnp.where(half == 0, across, pair)])
    far = swap(both, lambda x, y, z, c: (x, y ^ 3, z, c))
    plane = jnp.stack([both, far], axis=1)

    def along(array, k, second):
        return swap(
            array,
            lambda x, y, z, c: (x ^ k, y, z, c) if (c == 1) != second else (x, y, z ^ k, c),
        )

    order = (1, 3, 2)
    near = {k: along(plane, k, False) for k in order}
    line = [plane] + [near[k] for k in (1, 2, 3)]
    where = device.reshape(1)
    smem = pl.BlockSpec(memory_space=pltpu.SMEM)
    vmem = pl.BlockSpec(memory_space=pltpu.VMEM)
    positions = jax.ShapeDtypeStruct((2 * BLOCK, 128), jnp.int32)
    rows, first_pos, query_pos = pl.pallas_call(
        prepare,
        out_shape=(
            jax.ShapeDtypeStruct((HEADS * BLOCK, SIZE), jnp.bfloat16),
            positions,
            positions,
        ),
        in_specs=[smem, smem, vmem, pl.BlockSpec(memory_space=pl.ANY)],
        out_specs=(vmem,) * 3,
        compiler_params=pltpu.CompilerParams(vmem_limit_bytes=16 * 2**20),
    )(where, doc_lengths, queries, near[order[0]])
    other = swap(rows, lambda x, y, z, c: (x, y, z, 1 - c))
    pieces = {}
    for k in order:
        chosen = []
        for j in range(4):
            xr, zr = jnp.where(core == 0, x ^ k, x), jnp.where(core == 0, z, z ^ k)
            xs, zs = jnp.where(core == 0, x, x ^ j), jnp.where(core == 0, z ^ j, z)
            second = (half == 1) & (xs * 4 + zs < xr * 4 + zr)
            chosen.append(jnp.where(second, line[j][1], line[j][0]))
        pieces[k] = along(jnp.stack(chosen), k, True)
    scalars = [where, doc_lengths, first_pos, query_pos]
    rows, *sums = call("first", scalars, [rows, other], line)
    sums = call("middle", scalars, [rows, *sums], [pieces[1]])
    own, stat, sent, *_ = call(
        "last", scalars, [rows, *sums], [pieces[3], pieces[2], pieces[1], *line]
    )
    got = swap(sent, lambda x, y, z, c: (x, y, z, 1 - c))
    return pl.pallas_call(
        merge,
        out_shape=jax.ShapeDtypeStruct(queries.shape, jnp.bfloat16),
        in_specs=[vmem] * 3,
        out_specs=vmem,
        compiler_params=pltpu.CompilerParams(vmem_limit_bytes=16 * 2**20),
    )(own, stat, got)


def solution(mesh):
    in_specs = (P(AXES, None), P(AXES, None), P(AXES, None), P())
    return jax.shard_map(
        body, mesh=mesh, in_specs=in_specs, out_specs=P(AXES, None), check_vma=False
    )
```

```python
import functools
import math

import jax
import jax.numpy as jnp
from jax import lax
from jax.experimental import pallas as pl
from jax.experimental.pallas import tpu as pltpu
from jax.sharding import PartitionSpec as P

AXES = ("outer", "inner")
HEADS = 12
SIZE = 128
BLOCK = 128
SCALE = math.log2(math.e) / math.sqrt(SIZE)
MASKED = -1e30
EMPTY = -1e20
LEAST = 2.0**-80
MOST = 2.0**100
AFTER = 1 << 20
SIDES = 1
STEP = 4


def number(x, y, z, core):
    return ((y % 2) * 4 + x) * 16 + z * 4 + (y // 2) * 2 + core


def swap(array, partner):
    pairs = [
        (number(a, b, c, d), number(*partner(a, b, c, d)))
        for a in range(4)
        for b in range(4)
        for c in range(4)
        for d in range(2)
    ]
    return lax.ppermute(array, AXES, pairs)


def place(device):
    return device // 64, (device // 16) % 4, (device // 4) % 4, (device // 2) % 2, device % 2


def flag(condition):
    return jnp.where(condition, 1, 0).astype(jnp.int32)


def prepare(device_ref, docs_ref, own_ref, other_ref, unused_ref, rows, first_pos, query_pos):
    device = device_ref[0]
    chip = device // 2
    for h in range(HEADS):
        columns = slice(h * SIZE, (h + 1) * SIZE)
        rows[h * BLOCK : (h + 1) * BLOCK, :] = own_ref[:, columns]
        rows[(HEADS + h) * BLOCK : (HEADS + h + 1) * BLOCK, :] = other_ref[:, columns]
    token = lax.broadcasted_iota(jnp.int32, (2 * BLOCK, 128), 0)
    position = jnp.where(
        token < BLOCK, device * BLOCK + token, (chip * 4 + 1 - device) * BLOCK + token - BLOCK
    )
    start = jnp.zeros_like(position)
    end = jnp.int32(0)
    for j in range(docs_ref.shape[0]):
        end = end + docs_ref[j]
        start = jnp.where(position >= end, end, start)
    query_pos[...] = position
    first_pos[...] = start


def blocks_of(stage, pieces, spot):
    half, x, z, g, core = spot

    def base(chosen, xs, zs, gs):
        return ((chosen * 4 + xs) * 16 + zs * 4 + gs * 2 + core) * BLOCK

    blocks = []
    if stage == "first":
        own = pieces[0]
        across = half * flag((g ^ 1) > g)
        blocks.append((own[0, 0], base(half, x, z, g)))
        blocks.append((own[across, 1], base(half - across, x, z, g ^ 1)))
        for k in (1, 2, 3):
            xs, zs = jnp.where(core == 1, x, x ^ k), jnp.where(core == 1, z ^ k, z)
            across = half * flag(xs * 4 + zs > x * 4 + z)
            for r in range(2):
                blocks.append((pieces[k][across, r], base(half - across, xs, zs, g ^ r)))
        blocks.append((own[1, 0], base(1 - half, x, z, g)))
        return blocks
    for k, piece in zip((1,) if stage == "middle" else (3, 2), pieces, strict=True):
        for j in range(4):
            xs = jnp.where(core == 1, x ^ k, x ^ j)
            zs = jnp.where(core == 1, z ^ j, z ^ k)
            across = half * flag(xs * 4 + zs > x * 4 + z)
            for r in range(2):
                blocks.append((piece[j, r], base(half - across, xs, zs, g ^ r)))
    return blocks


def attend(stage, *refs):
    refs = list(refs)
    device_ref, docs_ref, first_pos, query_pos = refs[:4]
    refs = refs[4:]
    if stage == "first":
        rows, pieces, refs = refs[0], refs[1:5], refs[5:]
        total, accum = refs[:2]
        window, bias, base_ref = refs[2:]
    else:
        rows, total_in, accum_in = refs[:3]
        refs = refs[3:]
        count = {"middle": 1, "last": 7}[stage]
        pieces, refs = refs[:count], refs[count:]
        if stage == "last":
            own_out, own_stat, sent = refs[:3]
            refs = refs[3:]
        total, accum = refs[:2]
        window, bias, base_ref = refs[2:5]
    device = device_ref[0]
    spot = place(device)
    chip = device // 2

    lowest, highest = chip * 2 * BLOCK, chip * 2 * BLOCK + 2 * BLOCK - 1
    low_start, high_start, end = jnp.int32(0), jnp.int32(0), jnp.int32(0)
    for j in range(docs_ref.shape[0]):
        end = end + docs_ref[j]
        low_start = jnp.where(lowest >= end, end, low_start)
        high_start = jnp.where(highest >= end, end, high_start)
    def fill(blocks):
        for i, (values, begin) in enumerate(blocks):
            window[i * BLOCK : (i + 1) * BLOCK, :] = values
            base_ref[i] = begin

    def needed(first, count):
        some, every = jnp.int32(0), jnp.int32(1)
        for j in range(count):
            begin = base_ref[first + j]
            some = some | flag((begin <= highest) & (begin + BLOCK - 1 >= low_start))
            every = every & flag((begin + BLOCK - 1 <= lowest) & (begin >= high_start))
        return some, every

    def mask(first, count):
        lane = lax.broadcasted_iota(jnp.int32, (2 * BLOCK, 128), 1)
        for j in range(count):
            key_pos = lane + base_ref[first + j]
            allowed = (key_pos >= first_pos[...]) & (key_pos <= query_pos[...])
            bias[:, j * 128 : (j + 1) * 128] = jnp.where(allowed, 0.0, MASKED)

    def offset_of(first):
        return first * BLOCK if isinstance(first, int) else pl.multiple_of(first * BLOCK, BLOCK)

    def tile(first, count, masked, initial):
        width = count * BLOCK
        key = window[pl.ds(offset_of(first), width), 0:128]
        value = window[pl.ds(offset_of(first), width), 128:256]
        for side in range(SIDES):
            size = 2 * HEADS * BLOCK // SIDES
            span = slice(side * size, (side + 1) * size)
            scores = lax.dot_general(
                rows[span, :], key, (((1,), (1,)), ((), ())), preferred_element_type=jnp.float32
            )
            scores = scores * SCALE
            if masked:
                left, right = bias[:BLOCK, :width], bias[BLOCK:, :width]
                spread = ([left] * HEADS + [right] * HEADS)[
                    span.start // BLOCK : span.stop // BLOCK
                ]
                scores = scores + jnp.concatenate(spread, axis=0)
            weights = jnp.exp2(scores)
            part = weights[:, 0:128]
            for j in range(1, count):
                part = part + weights[:, j * 128 : (j + 1) * 128]
            product = jnp.dot(
                weights.astype(jnp.bfloat16), value, preferred_element_type=jnp.float32
            )
            if not initial:
                total[span, :] = total[span, :] + part
                accum[span, :] = accum[span, :] + product
            elif stage == "first":
                total[span, :] = part
                accum[span, :] = product
            else:
                total[span, :] = total_in[span, :] + part
                accum[span, :] = accum_in[span, :] + product

    def step(first, count, initial):
        some, every = needed(first, count)

        @pl.when((some == 1) & (every == 1))
        def _():
            tile(first, count, False, initial)

        @pl.when((some == 1) & (every == 0))
        def _():
            mask(first, count)
            tile(first, count, True, initial)

        if initial:

            @pl.when(some == 0)
            def _():
                if stage == "first":
                    total[...] = jnp.zeros_like(total)
                    accum[...] = jnp.zeros_like(accum)
                else:
                    total[...] = total_in[...]
                    accum[...] = accum_in[...]

    def advance(i, carry):
        step(i * STEP, STEP, False)
        return carry

    blocks = blocks_of(stage, pieces[:2] if stage == "last" else pieces, spot)
    fill(blocks)
    step(0, STEP, True)
    lax.fori_loop(1, len(blocks) // STEP, advance, 0)
    if len(blocks) % STEP:
        step(len(blocks) - 1, 1, False)
    if stage != "last":
        return

    top = refs[5]

    def finish(shifted):
        lane = lax.broadcasted_iota(jnp.int32, (BLOCK, 128), 1)
        bad = jnp.zeros((BLOCK, 1), jnp.int32)
        stats = []
        for side in range(2):
            stat = jnp.zeros((BLOCK, 128), jnp.float32)
            for h in range(HEADS):
                columns = slice(h * SIZE, (h + 1) * SIZE)
                span = slice((side * HEADS + h) * BLOCK, (side * HEADS + h + 1) * BLOCK)
                held = jnp.sum(total[span, :], axis=1, keepdims=True)
                fine = (held >= LEAST) & (held <= MOST)
                if side == 1:
                    fine = fine | (first_pos[BLOCK:, 0:1] >= (chip * 4 + 1 - device) * BLOCK)
                bad = jnp.where(fine, bad, 1)
                filled = held > 0.0
                divisor = jnp.where(filled, held, 1.0)
                level = jnp.log2(divisor)
                if shifted:
                    level = level + top[span, :]
                stat = jnp.where(lane == h, jnp.where(filled, level, EMPTY), stat)
                result = accum[span, :] * (1.0 / divisor)
                if side == 0:
                    own_out[:, columns] = result
                else:
                    sent[:, columns] = result.astype(jnp.bfloat16)
            stats.append(stat)
        own_stat[...] = stats[0]
        rest = stats[1]
        high = rest.astype(jnp.bfloat16)
        rest = rest - high.astype(jnp.float32)
        middle = rest.astype(jnp.bfloat16)
        low = (rest - middle.astype(jnp.float32)).astype(jnp.bfloat16)
        base_column = HEADS * SIZE
        sent[:, base_column : base_column + 128] = high
        sent[:, base_column + 128 : base_column + 256] = middle
        sent[:, base_column + 256 : base_column + 384] = low
        return jnp.max(bad)

    bad = finish(False)

    @pl.when(bad > 0)
    def _():
        top[...] = jnp.full_like(top, EMPTY)
        total[...] = jnp.zeros_like(total)
        accum[...] = jnp.zeros_like(accum)
        width = STEP * BLOCK

        def careful(i, carry):
            first = i * STEP
            mask(first, STEP)
            key = window[pl.ds(offset_of(first), width), 0:128]
            value = window[pl.ds(offset_of(first), width), 128:256]

            def head(t, carry):
                span = pl.ds(pl.multiple_of(t * BLOCK, BLOCK), BLOCK)
                side = pl.ds(pl.multiple_of(t // HEADS * BLOCK, BLOCK), BLOCK)
                scores = lax.dot_general(
                    rows[span, :],
                    key,
                    (((1,), (1,)), ((), ())),
                    preferred_element_type=jnp.float32,
                )
                scores = scores * SCALE + bias[side, :width]
                before = top[span, :]
                fresh = jnp.maximum(before, jnp.max(scores, axis=1, keepdims=True))
                weights = jnp.exp2(scores - jnp.concatenate([fresh] * STEP, axis=1))
                part = weights[:, 0:128]
                for j in range(1, STEP):
                    part = part + weights[:, j * 128 : (j + 1) * 128]
                factor = jnp.exp2(before - fresh)
                total[span, :] = total[span, :] * factor + part
                accum[span, :] = accum[span, :] * factor + jnp.dot(
                    weights.astype(jnp.bfloat16), value, preferred_element_type=jnp.float32
                )
                top[span, :] = fresh
                return carry

            lax.fori_loop(0, 2 * HEADS, head, 0)
            return carry

        for name, group in (("first", pieces[3:7]), ("middle", pieces[2:3]), ("last", pieces[:2])):
            again = blocks_of(name, group, spot)
            while len(again) % STEP:
                again.append((again[0][0], jnp.int32(AFTER)))
            fill(again)
            lax.fori_loop(0, len(again) // STEP, careful, 0)
        finish(True)


def merge(own_ref, stat_ref, got_ref, out_ref):
    base_column = HEADS * SIZE
    other = (
        got_ref[:, base_column : base_column + 128].astype(jnp.float32)
        + got_ref[:, base_column + 128 : base_column + 256].astype(jnp.float32)
    ) + got_ref[:, base_column + 256 : base_column + 384].astype(jnp.float32)
    mine = stat_ref[...]
    peak = jnp.maximum(mine, other)
    left, right = jnp.exp2(mine - peak), jnp.exp2(other - peak)
    both = left + right
    left, right = left / both, right / both
    for h in range(HEADS):
        columns = slice(h * SIZE, (h + 1) * SIZE)
        out_ref[:, columns] = (
            own_ref[:, columns] * left[:, h : h + 1]
            + got_ref[:, columns].astype(jnp.float32) * right[:, h : h + 1]
        ).astype(jnp.bfloat16)


def call(stage, scalars, arrays, pieces):
    smem = pl.BlockSpec(memory_space=pltpu.SMEM)
    vmem = pl.BlockSpec(memory_space=pltpu.VMEM)
    tokens = 2 * BLOCK
    rows = HEADS * tokens
    shape = jax.ShapeDtypeStruct
    out_shape = (shape((rows, SIZE), jnp.float32),) * 2
    blocks = {"first": 9, "middle": 8, "last": 16}[stage]
    scratch_shapes = [
        pltpu.VMEM((blocks * BLOCK, 2 * SIZE), jnp.bfloat16),
        pltpu.VMEM((tokens, STEP * BLOCK), jnp.float32),
        pltpu.SMEM((blocks,), jnp.int32),
    ]
    aliases = {}
    if stage == "middle":
        aliases = {5: 0, 6: 1}
    if stage == "last":
        out_shape = (
            shape((BLOCK, HEADS * SIZE), jnp.float32),
            shape((BLOCK, 128), jnp.float32),
            shape((BLOCK, HEADS * SIZE + 384), jnp.bfloat16),
        ) + out_shape
        aliases = {5: 3, 6: 4}
        scratch_shapes.append(pltpu.VMEM((rows, 128), jnp.float32))
    work = rows * blocks * BLOCK
    return pl.pallas_call(
        functools.partial(attend, stage),
        out_shape=out_shape,
        in_specs=[smem, smem] + [vmem] * (2 + len(arrays) + len(pieces)),
        out_specs=(vmem,) * len(out_shape),
        scratch_shapes=scratch_shapes,
        input_output_aliases=aliases,
        compiler_params=pltpu.CompilerParams(vmem_limit_bytes=40 * 2**20),
        cost_estimate=pl.CostEstimate(
            flops=4 * work * SIZE, bytes_accessed=4 * 2**20, transcendentals=work
        ),
    )(*scalars, *arrays, *pieces)


def body(queries, keys, values, doc_lengths):
    device = lax.axis_index(AXES).astype(jnp.int32)
    half, x, z, g, core = place(device)
    pair = jnp.pad(keys, ((0, 0), (0, SIZE))) + jnp.pad(values, ((0, 0), (SIZE, 0)))
    beside = {k: swap(pair, lambda x, y, z, c, k=k: (x, y ^ k, z, c)) for k in (1, 3, 2)}
    other = swap(queries, lambda x, y, z, c: (x, y, z, 1 - c))
    mark = other[:, : 2 * SIZE]
    behind = jnp.where(mark == mark, beside[2], 0.0)
    plane = jnp.stack([jnp.stack([pair, behind]), jnp.stack([beside[1], beside[3]])])

    def along(array, k, second):
        return swap(
            array,
            lambda x, y, z, c: (x ^ k, y, z, c) if (c == 0) != second else (x, y, z ^ k, c),
        )

    order = (1, 3, 2)
    near = {k: along(plane, k, False) for k in order}
    line = [plane] + [near[k] for k in (1, 2, 3)]
    where = device.reshape(1)
    smem = pl.BlockSpec(memory_space=pltpu.SMEM)
    vmem = pl.BlockSpec(memory_space=pltpu.VMEM)
    positions = jax.ShapeDtypeStruct((2 * BLOCK, 128), jnp.int32)
    rows, first_pos, query_pos = pl.pallas_call(
        prepare,
        out_shape=(
            jax.ShapeDtypeStruct((2 * HEADS * BLOCK, SIZE), jnp.bfloat16),
            positions,
            positions,
        ),
        in_specs=[smem, smem, vmem, vmem, pl.BlockSpec(memory_space=pl.ANY)],
        out_specs=(vmem,) * 3,
        compiler_params=pltpu.CompilerParams(vmem_limit_bytes=16 * 2**20),
    )(where, doc_lengths, queries, other, near[order[0]])
    pieces = {}
    for k in order:
        chosen = []
        for j in range(4):
            xr, zr = jnp.where(core == 1, x ^ k, x), jnp.where(core == 1, z, z ^ k)
            xs, zs = jnp.where(core == 1, x, x ^ j), jnp.where(core == 1, z ^ j, z)
            across = (half == 1) & (xs * 4 + zs > xr * 4 + zr)
            chosen.append(jnp.where(across, line[j][1], line[j][0]))
        pieces[k] = along(jnp.stack(chosen), k, True)
    scalars = [where, doc_lengths, first_pos, query_pos]
    sums = call("first", scalars, [rows], line)
    sums = call("middle", scalars, [rows, *sums], [pieces[1]])
    own, stat, sent, *_ = call(
        "last", scalars, [rows, *sums], [pieces[3], pieces[2], pieces[1], *line]
    )
    got = swap(sent, lambda x, y, z, c: (x, y, z, 1 - c))
    return pl.pallas_call(
        merge,
        out_shape=jax.ShapeDtypeStruct(queries.shape, jnp.bfloat16),
        in_specs=[vmem] * 3,
        out_specs=vmem,
        compiler_params=pltpu.CompilerParams(vmem_limit_bytes=16 * 2**20),
    )(own, stat, got)


def solution(mesh):
    in_specs = (P(AXES, None), P(AXES, None), P(AXES, None), P())
    return jax.shard_map(
        body, mesh=mesh, in_specs=in_specs, out_specs=P(AXES, None), check_vma=False
    )
```

```python
import functools
import math

import jax
import jax.numpy as jnp
from jax import lax
from jax.experimental import pallas as pl
from jax.experimental.pallas import tpu as pltpu
from jax.sharding import PartitionSpec as P

AXES = ("outer", "inner")
HEADS = 12
SIZE = 128
BLOCK = 128
SCALE = math.log2(math.e) / math.sqrt(SIZE)
MASKED = -1e30
EMPTY = -1e20
LEAST = 2.0**-80
MOST = 2.0**100
AFTER = 1 << 20
SIDES = 1
STEP = 4


def number(x, y, z, core):
    return ((y % 2) * 4 + x) * 16 + z * 4 + (y // 2) * 2 + core


def swap(array, partner):
    pairs = [
        (number(a, b, c, d), number(*partner(a, b, c, d)))
        for a in range(4)
        for b in range(4)
        for c in range(4)
        for d in range(2)
    ]
    return lax.ppermute(array, AXES, pairs)


def place(device):
    return device // 64, (device // 16) % 4, (device // 4) % 4, (device // 2) % 2, device % 2


def flag(condition):
    return jnp.where(condition, 1, 0).astype(jnp.int32)


def prepare(device_ref, docs_ref, own_ref, other_ref, unused_ref, rows, first_pos, query_pos):
    device = device_ref[0]
    chip = device // 2
    for h in range(HEADS):
        columns = slice(h * SIZE, (h + 1) * SIZE)
        rows[h * BLOCK : (h + 1) * BLOCK, :] = own_ref[:, columns]
        rows[(HEADS + h) * BLOCK : (HEADS + h + 1) * BLOCK, :] = other_ref[:, columns]
    token = lax.broadcasted_iota(jnp.int32, (2 * BLOCK, 128), 0)
    position = jnp.where(
        token < BLOCK, device * BLOCK + token, (chip * 4 + 1 - device) * BLOCK + token - BLOCK
    )
    start = jnp.zeros_like(position)
    end = jnp.int32(0)
    for j in range(docs_ref.shape[0]):
        end = end + docs_ref[j]
        start = jnp.where(position >= end, end, start)
    query_pos[...] = position
    first_pos[...] = start


def blocks_of(stage, pieces, spot):
    half, x, z, g, core = spot

    def base(chosen, xs, zs, gs):
        return ((chosen * 4 + xs) * 16 + zs * 4 + gs * 2 + core) * BLOCK

    blocks = []
    if stage == "first":
        own = pieces[0]
        across = half * flag((g ^ 1) > g)
        blocks.append((own[0, 0], base(half, x, z, g)))
        blocks.append((own[across, 1], base(half - across, x, z, g ^ 1)))
        for k in (1, 2, 3):
            xs, zs = jnp.where(core == 1, x, x ^ k), jnp.where(core == 1, z ^ k, z)
            across = half * flag(xs * 4 + zs > x * 4 + z)
            for r in range(2):
                blocks.append((pieces[k][across, r], base(half - across, xs, zs, g ^ r)))
        blocks.append((own[1, 0], base(1 - half, x, z, g)))
        return blocks
    for k, piece in zip((1,) if stage == "middle" else (3, 2), pieces, strict=True):
        for j in range(4):
            xs = jnp.where(core == 1, x ^ k, x ^ j)
            zs = jnp.where(core == 1, z ^ j, z ^ k)
            across = half * flag(xs * 4 + zs > x * 4 + z)
            for r in range(2):
                blocks.append((piece[j, r], base(half - across, xs, zs, g ^ r)))
    return blocks


def attend(stage, *refs):
    refs = list(refs)
    device_ref, docs_ref, first_pos, query_pos = refs[:4]
    refs = refs[4:]
    if stage == "first":
        rows, pieces, refs = refs[0], refs[1:5], refs[5:]
        total, accum = refs[:2]
        window, bias, base_ref = refs[2:]
    else:
        rows, total_in, accum_in = refs[:3]
        refs = refs[3:]
        count = {"middle": 1, "last": 7}[stage]
        pieces, refs = refs[:count], refs[count:]
        if stage == "last":
            own_out, own_stat, sent = refs[:3]
            refs = refs[3:]
        total, accum = refs[:2]
        window, bias, base_ref = refs[2:5]
    device = device_ref[0]
    spot = place(device)
    chip = device // 2

    lowest, highest = chip * 2 * BLOCK, chip * 2 * BLOCK + 2 * BLOCK - 1
    low_start, high_start, end = jnp.int32(0), jnp.int32(0), jnp.int32(0)
    for j in range(docs_ref.shape[0]):
        end = end + docs_ref[j]
        low_start = jnp.where(lowest >= end, end, low_start)
        high_start = jnp.where(highest >= end, end, high_start)
    def fill(blocks):
        for i, (values, begin) in enumerate(blocks):
            window[i * BLOCK : (i + 1) * BLOCK, :] = values
            base_ref[i] = begin

    def needed(first, count):
        some, every = jnp.int32(0), jnp.int32(1)
        for j in range(count):
            begin = base_ref[first + j]
            some = some | flag((begin <= highest) & (begin + BLOCK - 1 >= low_start))
            every = every & flag((begin + BLOCK - 1 <= lowest) & (begin >= high_start))
        return some, every

    def mask(first, count):
        lane = lax.broadcasted_iota(jnp.int32, (2 * BLOCK, 128), 1)
        for j in range(count):
            key_pos = lane + base_ref[first + j]
            allowed = (key_pos >= first_pos[...]) & (key_pos <= query_pos[...])
            bias[:, j * 128 : (j + 1) * 128] = jnp.where(allowed, 0.0, MASKED)

    def offset_of(first):
        return first * BLOCK if isinstance(first, int) else pl.multiple_of(first * BLOCK, BLOCK)

    def tile(first, count, masked, initial):
        width = count * BLOCK
        key = window[pl.ds(offset_of(first), width), 0:128]
        value = window[pl.ds(offset_of(first), width), 128:256]
        for side in range(SIDES):
            size = 2 * HEADS * BLOCK // SIDES
            span = slice(side * size, (side + 1) * size)
            scores = lax.dot_general(
                rows[span, :], key, (((1,), (1,)), ((), ())), preferred_element_type=jnp.float32
            )
            scores = scores * SCALE
            if masked:
                left, right = bias[:BLOCK, :width], bias[BLOCK:, :width]
                spread = ([left] * HEADS + [right] * HEADS)[
                    span.start // BLOCK : span.stop // BLOCK
                ]
                scores = scores + jnp.concatenate(spread, axis=0)
            weights = jnp.exp2(scores)
            part = weights[:, 0:128]
            for j in range(1, count):
                part = part + weights[:, j * 128 : (j + 1) * 128]
            product = jnp.dot(
                weights.astype(jnp.bfloat16), value, preferred_element_type=jnp.float32
            )
            if not initial:
                total[span, :] = total[span, :] + part
                accum[span, :] = accum[span, :] + product
            elif stage == "first":
                total[span, :] = part
                accum[span, :] = product
            else:
                total[span, :] = total_in[span, :] + part
                accum[span, :] = accum_in[span, :] + product

    def step(first, count, initial):
        some, every = needed(first, count)

        @pl.when((some == 1) & (every == 1))
        def _():
            tile(first, count, False, initial)

        @pl.when((some == 1) & (every == 0))
        def _():
            mask(first, count)
            tile(first, count, True, initial)

        if initial:

            @pl.when(some == 0)
            def _():
                if stage == "first":
                    total[...] = jnp.zeros_like(total)
                    accum[...] = jnp.zeros_like(accum)
                else:
                    total[...] = total_in[...]
                    accum[...] = accum_in[...]

    def advance(i, carry):
        step(i * STEP, STEP, False)
        return carry

    blocks = blocks_of(stage, pieces[:2] if stage == "last" else pieces, spot)
    fill(blocks)
    step(0, STEP, True)
    lax.fori_loop(1, len(blocks) // STEP, advance, 0)
    if len(blocks) % STEP:
        step(len(blocks) - 1, 1, False)
    if stage != "last":
        return

    top = refs[5]

    def finish(shifted):
        lane = lax.broadcasted_iota(jnp.int32, (BLOCK, 128), 1)
        bad = jnp.zeros((BLOCK, 1), jnp.int32)
        stats = []
        for side in range(2):
            stat = jnp.zeros((BLOCK, 128), jnp.float32)
            for h in range(HEADS):
                columns = slice(h * SIZE, (h + 1) * SIZE)
                span = slice((side * HEADS + h) * BLOCK, (side * HEADS + h + 1) * BLOCK)
                held = jnp.sum(total[span, :], axis=1, keepdims=True)
                fine = (held >= LEAST) & (held <= MOST)
                if side == 1:
                    fine = fine | (first_pos[BLOCK:, 0:1] >= (chip * 4 + 1 - device) * BLOCK)
                bad = jnp.where(fine, bad, 1)
                filled = held > 0.0
                divisor = jnp.where(filled, held, 1.0)
                level = jnp.log2(divisor)
                if shifted:
                    level = level + top[span, :]
                stat = jnp.where((lane & 15) == h, jnp.where(filled, level, EMPTY), stat)
                result = accum[span, :] * (1.0 / divisor)
                if side == 0:
                    own_out[:, columns] = result
                else:
                    sent[:, columns] = result.astype(jnp.bfloat16)
            stats.append(stat)
        own_stat[...] = stats[0]
        rest = stats[1]
        high = rest.astype(jnp.bfloat16)
        rest = rest - high.astype(jnp.float32)
        middle = rest.astype(jnp.bfloat16)
        low = (rest - middle.astype(jnp.float32)).astype(jnp.bfloat16)
        base_column = HEADS * SIZE
        terms = jnp.where(lane < 32, middle.astype(jnp.float32), low.astype(jnp.float32))
        terms = jnp.where(lane < 16, high.astype(jnp.float32), terms)
        sent[:, base_column : base_column + 128] = terms.astype(jnp.bfloat16)
        return jnp.max(bad)

    bad = finish(False)

    @pl.when(bad > 0)
    def _():
        top[...] = jnp.full_like(top, EMPTY)
        total[...] = jnp.zeros_like(total)
        accum[...] = jnp.zeros_like(accum)
        width = STEP * BLOCK

        def careful(i, carry):
            first = i * STEP
            mask(first, STEP)
            key = window[pl.ds(offset_of(first), width), 0:128]
            value = window[pl.ds(offset_of(first), width), 128:256]

            def head(t, carry):
                span = pl.ds(pl.multiple_of(t * BLOCK, BLOCK), BLOCK)
                side = pl.ds(pl.multiple_of(t // HEADS * BLOCK, BLOCK), BLOCK)
                scores = lax.dot_general(
                    rows[span, :],
                    key,
                    (((1,), (1,)), ((), ())),
                    preferred_element_type=jnp.float32,
                )
                scores = scores * SCALE + bias[side, :width]
                before = top[span, :]
                fresh = jnp.maximum(before, jnp.max(scores, axis=1, keepdims=True))
                weights = jnp.exp2(scores - jnp.concatenate([fresh] * STEP, axis=1))
                part = weights[:, 0:128]
                for j in range(1, STEP):
                    part = part + weights[:, j * 128 : (j + 1) * 128]
                factor = jnp.exp2(before - fresh)
                total[span, :] = total[span, :] * factor + part
                accum[span, :] = accum[span, :] * factor + jnp.dot(
                    weights.astype(jnp.bfloat16), value, preferred_element_type=jnp.float32
                )
                top[span, :] = fresh
                return carry

            lax.fori_loop(0, 2 * HEADS, head, 0)
            return carry

        for name, group in (("first", pieces[3:7]), ("middle", pieces[2:3]), ("last", pieces[:2])):
            again = blocks_of(name, group, spot)
            while len(again) % STEP:
                again.append((again[0][0], jnp.int32(AFTER)))
            fill(again)
            lax.fori_loop(0, len(again) // STEP, careful, 0)
        finish(True)


def merge(own_ref, stat_ref, got_ref, out_ref):
    base_column = HEADS * SIZE
    terms = got_ref[:, base_column : base_column + 128].astype(jnp.float32)
    other = (terms + pltpu.roll(terms, 112, 1)) + pltpu.roll(terms, 96, 1)
    mine = stat_ref[...]
    peak = jnp.maximum(mine, other)
    left, right = jnp.exp2(mine - peak), jnp.exp2(other - peak)
    both = left + right
    left, right = left / both, right / both
    for h in range(HEADS):
        columns = slice(h * SIZE, (h + 1) * SIZE)
        out_ref[:, columns] = (
            own_ref[:, columns] * left[:, h : h + 1]
            + got_ref[:, columns].astype(jnp.float32) * right[:, h : h + 1]
        ).astype(jnp.bfloat16)


def call(stage, scalars, arrays, pieces):
    smem = pl.BlockSpec(memory_space=pltpu.SMEM)
    vmem = pl.BlockSpec(memory_space=pltpu.VMEM)
    tokens = 2 * BLOCK
    rows = HEADS * tokens
    shape = jax.ShapeDtypeStruct
    out_shape = (shape((rows, SIZE), jnp.float32),) * 2
    blocks = {"first": 9, "middle": 8, "last": 16}[stage]
    scratch_shapes = [
        pltpu.VMEM((blocks * BLOCK, 2 * SIZE), jnp.bfloat16),
        pltpu.VMEM((tokens, STEP * BLOCK), jnp.float32),
        pltpu.SMEM((blocks,), jnp.int32),
    ]
    aliases = {}
    if stage == "middle":
        aliases = {5: 0, 6: 1}
    if stage == "last":
        out_shape = (
            shape((BLOCK, HEADS * SIZE), jnp.float32),
            shape((BLOCK, 128), jnp.float32),
            shape((BLOCK, HEADS * SIZE + 128), jnp.bfloat16),
        ) + out_shape
        aliases = {5: 3, 6: 4}
        scratch_shapes.append(pltpu.VMEM((rows, 128), jnp.float32))
    work = rows * blocks * BLOCK
    return pl.pallas_call(
        functools.partial(attend, stage),
        out_shape=out_shape,
        in_specs=[smem, smem] + [vmem] * (2 + len(arrays) + len(pieces)),
        out_specs=(vmem,) * len(out_shape),
        scratch_shapes=scratch_shapes,
        input_output_aliases=aliases,
        compiler_params=pltpu.CompilerParams(vmem_limit_bytes=40 * 2**20),
        cost_estimate=pl.CostEstimate(
            flops=4 * work * SIZE, bytes_accessed=4 * 2**20, transcendentals=work
        ),
    )(*scalars, *arrays, *pieces)


def body(queries, keys, values, doc_lengths):
    device = lax.axis_index(AXES).astype(jnp.int32)
    half, x, z, g, core = place(device)
    pair = jnp.pad(keys, ((0, 0), (0, SIZE))) + jnp.pad(values, ((0, 0), (SIZE, 0)))
    beside = {k: swap(pair, lambda x, y, z, c, k=k: (x, y ^ k, z, c)) for k in (2, 1, 3)}
    other = swap(queries, lambda x, y, z, c: (x, y, z, 1 - c))
    mark = other[:, : 2 * SIZE]
    behind = jnp.where(mark == mark, beside[2], 0.0)
    plane = jnp.stack([jnp.stack([pair, behind]), jnp.stack([beside[1], beside[3]])])

    def along(array, k, second):
        return swap(
            array,
            lambda x, y, z, c: (x ^ k, y, z, c) if (c == 0) != second else (x, y, z ^ k, c),
        )

    order = (1, 3, 2)
    near = {k: along(plane, k, False) for k in order}
    line = [plane] + [near[k] for k in (1, 2, 3)]
    where = device.reshape(1)
    smem = pl.BlockSpec(memory_space=pltpu.SMEM)
    vmem = pl.BlockSpec(memory_space=pltpu.VMEM)
    positions = jax.ShapeDtypeStruct((2 * BLOCK, 128), jnp.int32)
    rows, first_pos, query_pos = pl.pallas_call(
        prepare,
        out_shape=(
            jax.ShapeDtypeStruct((2 * HEADS * BLOCK, SIZE), jnp.bfloat16),
            positions,
            positions,
        ),
        in_specs=[smem, smem, vmem, vmem, pl.BlockSpec(memory_space=pl.ANY)],
        out_specs=(vmem,) * 3,
        compiler_params=pltpu.CompilerParams(vmem_limit_bytes=16 * 2**20),
    )(where, doc_lengths, queries, other, near[order[0]])
    pieces = {}
    for k in order:
        chosen = []
        for j in range(4):
            xr, zr = jnp.where(core == 1, x ^ k, x), jnp.where(core == 1, z, z ^ k)
            xs, zs = jnp.where(core == 1, x, x ^ j), jnp.where(core == 1, z ^ j, z)
            across = (half == 1) & (xs * 4 + zs > xr * 4 + zr)
            chosen.append(jnp.where(across, line[j][1], line[j][0]))
        pieces[k] = along(jnp.stack(chosen), k, True)
    scalars = [where, doc_lengths, first_pos, query_pos]
    sums = call("first", scalars, [rows], line)
    sums = call("middle", scalars, [rows, *sums], [pieces[1]])
    own, stat, sent, *_ = call(
        "last", scalars, [rows, *sums], [pieces[3], pieces[2], pieces[1], *line]
    )
    got = swap(sent, lambda x, y, z, c: (x, y, z, 1 - c))
    return pl.pallas_call(
        merge,
        out_shape=jax.ShapeDtypeStruct(queries.shape, jnp.bfloat16),
        in_specs=[vmem] * 3,
        out_specs=vmem,
        compiler_params=pltpu.CompilerParams(vmem_limit_bytes=16 * 2**20),
    )(own, stat, got)


def solution(mesh):
    in_specs = (P(AXES, None), P(AXES, None), P(AXES, None), P())
    return jax.shard_map(
        body, mesh=mesh, in_specs=in_specs, out_specs=P(AXES, None), check_vma=False
    )
```

```python
import functools
import math

import jax
import jax.numpy as jnp
from jax import lax
from jax.experimental import pallas as pl
from jax.experimental.pallas import tpu as pltpu
from jax.sharding import PartitionSpec as P

AXES = ("outer", "inner")
HEADS = 12
SIZE = 128
BLOCK = 128
SCALE = math.log2(math.e) / math.sqrt(SIZE)
MASKED = -1e30
EMPTY = -1e20
LEAST = 2.0**-80
MOST = 2.0**100
AFTER = 1 << 20
SIDES = 2
STEP = 4


def number(x, y, z, core):
    return ((y % 2) * 4 + x) * 16 + z * 4 + (y // 2) * 2 + core


def swap(array, partner):
    pairs = [
        (number(a, b, c, d), number(*partner(a, b, c, d)))
        for a in range(4)
        for b in range(4)
        for c in range(4)
        for d in range(2)
    ]
    return lax.ppermute(array, AXES, pairs)


def place(device):
    return device // 64, (device // 16) % 4, (device // 4) % 4, (device // 2) % 2, device % 2


def flag(condition):
    return jnp.where(condition, 1, 0).astype(jnp.int32)


def prepare(device_ref, docs_ref, own_ref, other_ref, unused_ref, rows, first_pos, query_pos):
    device = device_ref[0]
    chip = device // 2
    for h in range(HEADS):
        columns = slice(h * SIZE, (h + 1) * SIZE)
        rows[h * BLOCK : (h + 1) * BLOCK, :] = own_ref[:, columns]
        rows[(HEADS + h) * BLOCK : (HEADS + h + 1) * BLOCK, :] = other_ref[:, columns]
    token = lax.broadcasted_iota(jnp.int32, (2 * BLOCK, 128), 0)
    position = jnp.where(
        token < BLOCK, device * BLOCK + token, (chip * 4 + 1 - device) * BLOCK + token - BLOCK
    )
    start = jnp.zeros_like(position)
    end = jnp.int32(0)
    for j in range(docs_ref.shape[0]):
        end = end + docs_ref[j]
        start = jnp.where(position >= end, end, start)
    query_pos[...] = position
    first_pos[...] = start


def blocks_of(stage, pieces, spot):
    half, x, z, g, core = spot

    def base(chosen, xs, zs, gs):
        return ((chosen * 4 + xs) * 16 + zs * 4 + gs * 2 + core) * BLOCK

    blocks = []
    if stage == "first":
        own = pieces[0]
        across = half * flag((g ^ 1) > g)
        blocks.append((own[0, 0], base(half, x, z, g)))
        blocks.append((own[across, 1], base(half - across, x, z, g ^ 1)))
        for k in (1, 2, 3):
            xs, zs = jnp.where(core == 1, x, x ^ k), jnp.where(core == 1, z ^ k, z)
            across = half * flag(xs * 4 + zs > x * 4 + z)
            for r in range(2):
                blocks.append((pieces[k][across, r], base(half - across, xs, zs, g ^ r)))
        blocks.append((own[1, 0], base(1 - half, x, z, g)))
        return blocks
    for k, piece in zip((1,) if stage == "middle" else (3, 2), pieces, strict=True):
        for j in range(4):
            xs = jnp.where(core == 1, x ^ k, x ^ j)
            zs = jnp.where(core == 1, z ^ j, z ^ k)
            across = half * flag(xs * 4 + zs > x * 4 + z)
            for r in range(2):
                blocks.append((piece[j, r], base(half - across, xs, zs, g ^ r)))
    return blocks


def attend(stage, *refs):
    refs = list(refs)
    device_ref, docs_ref, first_pos, query_pos = refs[:4]
    refs = refs[4:]
    if stage == "first":
        rows, pieces, refs = refs[0], refs[1:5], refs[5:]
        total, accum = refs[:2]
        window, bias, base_ref = refs[2:]
    else:
        rows, total_in, accum_in = refs[:3]
        refs = refs[3:]
        count = {"middle": 1, "last": 7}[stage]
        pieces, refs = refs[:count], refs[count:]
        if stage == "last":
            own_out, own_stat, sent = refs[:3]
            refs = refs[3:]
        total, accum = refs[:2]
        window, bias, base_ref = refs[2:5]
    device = device_ref[0]
    spot = place(device)
    chip = device // 2

    lowest, highest = chip * 2 * BLOCK, chip * 2 * BLOCK + 2 * BLOCK - 1
    low_start, high_start, end = jnp.int32(0), jnp.int32(0), jnp.int32(0)
    for j in range(docs_ref.shape[0]):
        end = end + docs_ref[j]
        low_start = jnp.where(lowest >= end, end, low_start)
        high_start = jnp.where(highest >= end, end, high_start)
    def fill(blocks):
        for i, (values, begin) in enumerate(blocks):
            window[i * BLOCK : (i + 1) * BLOCK, :] = values
            base_ref[i] = begin

    def needed(first, count):
        some, every = jnp.int32(0), jnp.int32(1)
        for j in range(count):
            begin = base_ref[first + j]
            some = some | flag((begin <= highest) & (begin + BLOCK - 1 >= low_start))
            every = every & flag((begin + BLOCK - 1 <= lowest) & (begin >= high_start))
        return some, every

    def mask(first, count):
        lane = lax.broadcasted_iota(jnp.int32, (2 * BLOCK, 128), 1)
        for j in range(count):
            key_pos = lane + base_ref[first + j]
            allowed = (key_pos >= first_pos[...]) & (key_pos <= query_pos[...])
            bias[:, j * 128 : (j + 1) * 128] = jnp.where(allowed, 0.0, MASKED)

    def offset_of(first):
        return first * BLOCK if isinstance(first, int) else pl.multiple_of(first * BLOCK, BLOCK)

    def tile(first, count, masked, initial):
        width = count * BLOCK
        key = window[pl.ds(offset_of(first), width), 0:128]
        value = window[pl.ds(offset_of(first), width), 128:256]
        for side in range(SIDES):
            size = 2 * HEADS * BLOCK // SIDES
            span = slice(side * size, (side + 1) * size)
            scores = lax.dot_general(
                rows[span, :], key, (((1,), (1,)), ((), ())), preferred_element_type=jnp.float32
            )
            scores = scores * SCALE
            if masked:
                left, right = bias[:BLOCK, :width], bias[BLOCK:, :width]
                spread = ([left] * HEADS + [right] * HEADS)[
                    span.start // BLOCK : span.stop // BLOCK
                ]
                scores = scores + jnp.concatenate(spread, axis=0)
            weights = jnp.exp2(scores)
            part = weights[:, 0:128]
            for j in range(1, count):
                part = part + weights[:, j * 128 : (j + 1) * 128]
            product = jnp.dot(
                weights.astype(jnp.bfloat16), value, preferred_element_type=jnp.float32
            )
            if not initial:
                total[span, :] = total[span, :] + part
                accum[span, :] = accum[span, :] + product
            elif stage == "first":
                total[span, :] = part
                accum[span, :] = product
            else:
                total[span, :] = total_in[span, :] + part
                accum[span, :] = accum_in[span, :] + product

    def step(first, count, initial):
        some, every = needed(first, count)

        @pl.when((some == 1) & (every == 1))
        def _():
            tile(first, count, False, initial)

        @pl.when((some == 1) & (every == 0))
        def _():
            mask(first, count)
            tile(first, count, True, initial)

        if initial:

            @pl.when(some == 0)
            def _():
                if stage == "first":
                    total[...] = jnp.zeros_like(total)
                    accum[...] = jnp.zeros_like(accum)
                else:
                    total[...] = total_in[...]
                    accum[...] = accum_in[...]

    def advance(i, carry):
        step(i * STEP, STEP, False)
        return carry

    blocks = blocks_of(stage, pieces[:2] if stage == "last" else pieces, spot)
    fill(blocks)
    step(0, STEP, True)
    lax.fori_loop(1, len(blocks) // STEP, advance, 0)
    if len(blocks) % STEP:
        step(len(blocks) - 1, 1, False)
    if stage != "last":
        return

    top = refs[5]

    def finish(shifted):
        lane = lax.broadcasted_iota(jnp.int32, (BLOCK, 128), 1)
        bad = jnp.zeros((BLOCK, 1), jnp.int32)
        stats = []
        for side in range(2):
            stat = jnp.zeros((BLOCK, 128), jnp.float32)
            for h in range(HEADS):
                columns = slice(h * SIZE, (h + 1) * SIZE)
                span = slice((side * HEADS + h) * BLOCK, (side * HEADS + h + 1) * BLOCK)
                held = jnp.sum(total[span, :], axis=1, keepdims=True)
                fine = (held >= LEAST) & (held <= MOST)
                if side == 1:
                    fine = fine | (first_pos[BLOCK:, 0:1] >= (chip * 4 + 1 - device) * BLOCK)
                bad = jnp.where(fine, bad, 1)
                filled = held > 0.0
                divisor = jnp.where(filled, held, 1.0)
                level = jnp.log2(divisor)
                if shifted:
                    level = level + top[span, :]
                stat = jnp.where((lane & 15) == h, jnp.where(filled, level, EMPTY), stat)
                result = accum[span, :] * (1.0 / divisor)
                if side == 0:
                    own_out[:, columns] = result
                else:
                    sent[:, columns] = result.astype(jnp.bfloat16)
            stats.append(stat)
        own_stat[...] = stats[0]
        rest = stats[1]
        high = rest.astype(jnp.bfloat16)
        rest = rest - high.astype(jnp.float32)
        middle = rest.astype(jnp.bfloat16)
        low = (rest - middle.astype(jnp.float32)).astype(jnp.bfloat16)
        base_column = HEADS * SIZE
        terms = jnp.where(lane < 32, middle.astype(jnp.float32), low.astype(jnp.float32))
        terms = jnp.where(lane < 16, high.astype(jnp.float32), terms)
        sent[:, base_column : base_column + 128] = terms.astype(jnp.bfloat16)
        return jnp.max(bad)

    bad = finish(False)

    @pl.when(bad > 0)
    def _():
        top[...] = jnp.full_like(top, EMPTY)
        total[...] = jnp.zeros_like(total)
        accum[...] = jnp.zeros_like(accum)
        width = STEP * BLOCK

        def careful(i, carry):
            first = i * STEP
            mask(first, STEP)
            key = window[pl.ds(offset_of(first), width), 0:128]
            value = window[pl.ds(offset_of(first), width), 128:256]

            def head(t, carry):
                span = pl.ds(pl.multiple_of(t * BLOCK, BLOCK), BLOCK)
                side = pl.ds(pl.multiple_of(t // HEADS * BLOCK, BLOCK), BLOCK)
                scores = lax.dot_general(
                    rows[span, :],
                    key,
                    (((1,), (1,)), ((), ())),
                    preferred_element_type=jnp.float32,
                )
                scores = scores * SCALE + bias[side, :width]
                before = top[span, :]
                fresh = jnp.maximum(before, jnp.max(scores, axis=1, keepdims=True))
                weights = jnp.exp2(scores - jnp.concatenate([fresh] * STEP, axis=1))
                part = weights[:, 0:128]
                for j in range(1, STEP):
                    part = part + weights[:, j * 128 : (j + 1) * 128]
                factor = jnp.exp2(before - fresh)
                total[span, :] = total[span, :] * factor + part
                accum[span, :] = accum[span, :] * factor + jnp.dot(
                    weights.astype(jnp.bfloat16), value, preferred_element_type=jnp.float32
                )
                top[span, :] = fresh
                return carry

            lax.fori_loop(0, 2 * HEADS, head, 0)
            return carry

        for name, group in (("first", pieces[3:7]), ("middle", pieces[2:3]), ("last", pieces[:2])):
            again = blocks_of(name, group, spot)
            while len(again) % STEP:
                again.append((again[0][0], jnp.int32(AFTER)))
            fill(again)
            lax.fori_loop(0, len(again) // STEP, careful, 0)
        finish(True)


def merge(own_ref, stat_ref, got_ref, out_ref):
    base_column = HEADS * SIZE
    terms = got_ref[:, base_column : base_column + 128].astype(jnp.float32)
    other = (terms + pltpu.roll(terms, 112, 1)) + pltpu.roll(terms, 96, 1)
    mine = stat_ref[...]
    peak = jnp.maximum(mine, other)
    left, right = jnp.exp2(mine - peak), jnp.exp2(other - peak)
    both = left + right
    left, right = left / both, right / both
    for h in range(HEADS):
        columns = slice(h * SIZE, (h + 1) * SIZE)
        out_ref[:, columns] = (
            own_ref[:, columns] * left[:, h : h + 1]
            + got_ref[:, columns].astype(jnp.float32) * right[:, h : h + 1]
        ).astype(jnp.bfloat16)


def call(stage, scalars, arrays, pieces):
    smem = pl.BlockSpec(memory_space=pltpu.SMEM)
    vmem = pl.BlockSpec(memory_space=pltpu.VMEM)
    tokens = 2 * BLOCK
    rows = HEADS * tokens
    shape = jax.ShapeDtypeStruct
    out_shape = (shape((rows, SIZE), jnp.float32),) * 2
    blocks = {"first": 9, "middle": 8, "last": 16}[stage]
    scratch_shapes = [
        pltpu.VMEM((blocks * BLOCK, 2 * SIZE), jnp.bfloat16),
        pltpu.VMEM((tokens, STEP * BLOCK), jnp.float32),
        pltpu.SMEM((blocks,), jnp.int32),
    ]
    aliases = {}
    if stage == "middle":
        aliases = {5: 0, 6: 1}
    if stage == "last":
        out_shape = (
            shape((BLOCK, HEADS * SIZE), jnp.float32),
            shape((BLOCK, 128), jnp.float32),
            shape((BLOCK, HEADS * SIZE + 128), jnp.bfloat16),
        ) + out_shape
        aliases = {5: 3, 6: 4}
        scratch_shapes.append(pltpu.VMEM((rows, 128), jnp.float32))
    work = rows * blocks * BLOCK
    return pl.pallas_call(
        functools.partial(attend, stage),
        out_shape=out_shape,
        in_specs=[smem, smem] + [vmem] * (2 + len(arrays) + len(pieces)),
        out_specs=(vmem,) * len(out_shape),
        scratch_shapes=scratch_shapes,
        input_output_aliases=aliases,
        compiler_params=pltpu.CompilerParams(vmem_limit_bytes=40 * 2**20),
        cost_estimate=pl.CostEstimate(
            flops=4 * work * SIZE, bytes_accessed=4 * 2**20, transcendentals=work
        ),
    )(*scalars, *arrays, *pieces)


def body(queries, keys, values, doc_lengths):
    device = lax.axis_index(AXES).astype(jnp.int32)
    half, x, z, g, core = place(device)
    pair = jnp.pad(keys, ((0, 0), (0, SIZE))) + jnp.pad(values, ((0, 0), (SIZE, 0)))
    beside = {k: swap(pair, lambda x, y, z, c, k=k: (x, y ^ k, z, c)) for k in (2, 1, 3)}
    other = swap(queries, lambda x, y, z, c: (x, y, z, 1 - c))
    mark = other[:, : 2 * SIZE]
    behind = jnp.where(mark == mark, beside[2], 0.0)
    plane = jnp.stack([jnp.stack([pair, behind]), jnp.stack([beside[1], beside[3]])])

    def along(array, k, second):
        return swap(
            array,
            lambda x, y, z, c: (x ^ k, y, z, c) if (c == 0) != second else (x, y, z ^ k, c),
        )

    order = (1, 3, 2)
    near = {k: along(plane, k, False) for k in order}
    line = [plane] + [near[k] for k in (1, 2, 3)]
    where = device.reshape(1)
    smem = pl.BlockSpec(memory_space=pltpu.SMEM)
    vmem = pl.BlockSpec(memory_space=pltpu.VMEM)
    positions = jax.ShapeDtypeStruct((2 * BLOCK, 128), jnp.int32)
    rows, first_pos, query_pos = pl.pallas_call(
        prepare,
        out_shape=(
            jax.ShapeDtypeStruct((2 * HEADS * BLOCK, SIZE), jnp.bfloat16),
            positions,
            positions,
        ),
        in_specs=[smem, smem, vmem, vmem, pl.BlockSpec(memory_space=pl.ANY)],
        out_specs=(vmem,) * 3,
        compiler_params=pltpu.CompilerParams(vmem_limit_bytes=16 * 2**20),
    )(where, doc_lengths, queries, other, near[order[0]])
    pieces = {}
    for k in order:
        chosen = []
        for j in range(4):
            xr, zr = jnp.where(core == 1, x ^ k, x), jnp.where(core == 1, z, z ^ k)
            xs, zs = jnp.where(core == 1, x, x ^ j), jnp.where(core == 1, z ^ j, z)
            across = (half == 1) & (xs * 4 + zs > xr * 4 + zr)
            chosen.append(jnp.where(across, line[j][1], line[j][0]))
        pieces[k] = along(jnp.stack(chosen), k, True)
    scalars = [where, doc_lengths, first_pos, query_pos]
    sums = call("first", scalars, [rows], line)
    sums = call("middle", scalars, [rows, *sums], [pieces[1]])
    own, stat, sent, *_ = call(
        "last", scalars, [rows, *sums], [pieces[3], pieces[2], pieces[1], *line]
    )
    got = swap(sent, lambda x, y, z, c: (x, y, z, 1 - c))
    return pl.pallas_call(
        merge,
        out_shape=jax.ShapeDtypeStruct(queries.shape, jnp.bfloat16),
        in_specs=[vmem] * 3,
        out_specs=vmem,
        compiler_params=pltpu.CompilerParams(vmem_limit_bytes=16 * 2**20),
    )(own, stat, got)


def solution(mesh):
    in_specs = (P(AXES, None), P(AXES, None), P(AXES, None), P())
    return jax.shard_map(
        body, mesh=mesh, in_specs=in_specs, out_specs=P(AXES, None), check_vma=False
    )
```
